128 devices in a mesh: dp: 8 (over z, core), head: 16 (over y, x).
Axes of the slice: x: 4, y: 4, z: 4, core: 2. Of those that a mesh axis runs over, the one named last changes fastest.
Arguments:
- residual_patch_matrix: bfloat16 [16384, 2048], P(('dp', 'head')), may hold values from -6 to 6
- transfer_tallies: int32 [8, 8], P('dp'), may hold values from 1 to 3, as said below
- picture_membership: int32 [8, 16], P('dp'), may hold values from 0 to 3, never falling along the last dimension, each value on 1 to 8 neighbouring positions
- premix_rescale_vector: float32 [2048], replicated, may hold values from 0.1 to 1.9
- triple_projection_matrix: bfloat16 [2048, 6144], P(None, 'head'), may hold values from -0.125 to 0.125
- per_head_sharpness: float32 [16], P('head'), may hold values from 2 to 900
- headmerge_projection_matrix: bfloat16 [2048, 2048], replicated, may hold values from -0.125 to 0.125
- prefeed_rescale_vector: float32 [2048], replicated, may hold values from 0.1 to 1.9
- feedforward_expand_matrix: bfloat16 [2048, 8192], P(None, 'head'), may hold values from -0.125 to 0.125
- feedforward_contract_matrix: bfloat16 [8192, 2048], P('head'), may hold values from -0.0625 to 0.0625
Outputs:
- block_out: bfloat16 [24576, 2048], P(('dp', 'head'))
The draws below stay inside these ranges and needn't reach their ends.
Inputs may be any that keep to these rules, and one draw needn't show every extreme that they name: transfer_tallies[s, d] is the number of units every device of group s sends to group d; each row sums to 16; every row's largest entry is 3, and some destination group receives 3 units from every source group. `picture_membership`: ids never fall along a row; each id covers 1 to 8 consecutive units, one exactly 8.
All inputs are finite; a program needn't handle non-finite values.
Results may differ from the reference program's by a relative error of at most 0.014.
The reference program's roundings to bfloat16 on the way count: a program that leaves them out, or rounds other values in their place, can miss the bound.
Values may be sent and summed in bfloat16 or wider, within the bound.
No kernel may reach another device: no remote copies, remote signals or barrier semaphores. Data moves between devices by JAX's collectives and lax.ppermute only.
A program may use at most 128 MiB of HBM per device.

```python
import math
import jax
import jax.numpy as jnp
import numpy as np
from jax import lax

D = 2048
HEADS = 16
HEAD_DIM = 128
FF = 8192
TOK_DEV = 128
ROW_UNIT = 8
UNITS = 16
MOST = 3
CAP = 24
SEGS = 4
SEG_MOST = 8
TOKENS = 16384
N_DP = 8
N_HEAD = 16


def draw_transfer_tallies(key, part):
    key = jax.random.fold_in(key, 7)
    key_full, key_rows = jax.random.split(key)
    full_column = jax.random.randint(key_full, (), 0, N_DP)
    extra_units = UNITS - MOST - (N_DP - 1)
    room_each = MOST - 1

    def one_row(row_key):
        shuffled = jax.random.permutation(row_key, (N_DP - 1) * room_each)
        chosen = (shuffled < extra_units).astype(jnp.int32)
        return chosen.reshape(N_DP - 1, room_each).sum(axis=1).astype(jnp.int32) + 1
    per_column = jax.vmap(one_row)(jax.random.split(key_rows, N_DP))
    column_ids = jnp.arange(N_DP, dtype=jnp.int32)
    source_slot = jnp.clip(column_ids - (column_ids > full_column).astype(jnp.int32), 0, N_DP - 2)
    drawn_values = jnp.take(per_column, source_slot, axis=1)
    return jnp.where(column_ids[None, :] == full_column, MOST, drawn_values).astype(jnp.int32)


def draw_per_head_sharpness(key, part):
    key = jax.random.fold_in(key, 11)
    scales = jnp.exp(jax.random.uniform(key, (HEADS,), jnp.float32, jnp.log(2.0), jnp.log(16.0)))
    return scales.astype(jnp.float32)


def block_levels(own_key, dims, shards, low, largest):
    factor_of, own = 1.0, jax.random.fold_in(own_key, 6)
    for dim, blocks in shards:
        heights = jnp.exp(jax.random.uniform(jax.random.fold_in(own, dim), (blocks,), jnp.float32, low / len(shards), largest / len(shards)))
        factor_of = factor_of * jnp.repeat(heights, dims[dim] // blocks).reshape([-1 if axis == dim else 1 for axis in range(len(dims))])
    return factor_of


def profile(number_of, total, reach, slope):
    loads = [(1 << 20) // math.isqrt(rank ** slope) + 1 for rank in range(2, number_of + 1)]
    spare, holding = total - reach - (number_of - 1), [1] * (number_of - 1)
    while spare > 0:
        candidates = [i for i in range(number_of - 1) if holding[i] < reach]
        whole, budget = sum([loads[i] for i in candidates]), spare
        for i in candidates:
            addition = min(reach - holding[i], max(1, budget * loads[i] // whole), spare)
            holding[i] = holding[i] + addition
            spare = spare - addition
    return np.array([reach] + holding)


def uneven_parts(stream_key, count, total, reach, slope):
    if count == 2:
        one = jax.random.randint(stream_key, (), max(1, total - reach), min(reach, total - 1) + 1)
        return jnp.stack([one, total - one])
    tallies = jnp.asarray(profile(count, total, reach, slope), jnp.int32)
    twos = (count - 1) // 2
    giver, receiver = tallies[1:1 + 2 * twos:2], tallies[2:2 + 2 * twos:2]
    margin = jnp.minimum(giver - 1, reach - receiver)
    moved = jax.random.randint(jax.random.fold_in(stream_key, 1), (twos,), 0, 1 << 20) % (margin + 1)
    tallies = tallies.at[1:1 + 2 * twos:2].set(giver - moved).at[2:2 + 2 * twos:2].set(receiver + moved)
    return tallies[jax.random.permutation(jax.random.fold_in(stream_key, 2), count)]


def normal_values(stream_key, dims, width, bound, cuts=(), kind=jnp.bfloat16):
    array = width * jax.random.normal(stream_key, dims, jnp.float32)
    if cuts:
        array = array * block_levels(stream_key, dims, cuts, -0.22, 0.18)
    return jnp.clip(array, -bound, bound).astype(kind)


def setup_inputs(seed: int = 0) -> dict:
    streams_of = jax.random.split(jax.random.key(seed), 11)
    return {
        "residual_patch_matrix": normal_values(streams_of[0], (TOKENS, D), 1.0, 6.0, ((0, 128),)),
        "transfer_tallies": draw_transfer_tallies(jax.random.fold_in(streams_of[10], 71), 0),
        "picture_membership": jax.vmap(lambda own: jnp.searchsorted(jnp.cumsum(uneven_parts(own, SEGS, UNITS, SEG_MOST, 1)), jnp.arange(UNITS), side="right"))(jax.random.split(streams_of[2], N_DP)).reshape((N_DP, UNITS)).astype(jnp.int32),
        "premix_rescale_vector": jnp.clip(1.0 + 0.18 * jax.random.normal(streams_of[3], (D,), jnp.float32), 0.1, 1.9),
        "triple_projection_matrix": normal_values(streams_of[4], (D, 3 * D), D ** -0.5, 0.125, ((1, 16),)),
        "per_head_sharpness": draw_per_head_sharpness(jax.random.fold_in(streams_of[10], 71), 0),
        "headmerge_projection_matrix": normal_values(streams_of[6], (D, D), D ** -0.5, 0.125),
        "prefeed_rescale_vector": jnp.clip(1.0 + 0.18 * jax.random.normal(streams_of[7], (D,), jnp.float32), 0.1, 1.9),
        "feedforward_expand_matrix": normal_values(streams_of[8], (D, FF), D ** -0.5, 0.125, ((1, 16),)),
        "feedforward_contract_matrix": normal_values(streams_of[9], (FF, D), FF ** -0.5, 0.0625, ((0, 16),)),
    }


eps = 1e-06

def rms_scale(values, gain_vector):
    mean_square = lax.optimization_barrier(jnp.mean(values * values, axis=-1, keepdims=True))
    return values * lax.rsqrt(mean_square + eps) * gain_vector

def unit_norm(values):
    mean_square = lax.optimization_barrier(jnp.mean(values * values, axis=-1, keepdims=True))
    return values * lax.rsqrt(mean_square + eps) * values.shape[-1] ** (-0.5)

def shape_qkv(raw_qkv):
    row_count = raw_qkv.shape[0]
    grouped = raw_qkv.reshape(row_count, -1, 3, HEAD_DIM)
    query_part = unit_norm(grouped[:, :, 0])
    key_part = unit_norm(grouped[:, :, 1])
    stacked = jnp.stack([query_part, key_part, grouped[:, :, 2]], axis=2)
    return stacked.astype(jnp.bfloat16).reshape(row_count, -1)

def send_rows(count_row):
    offsets = (jnp.cumsum(count_row) - count_row).astype(jnp.int32)
    slot_index = jnp.arange(CAP, dtype=jnp.int32)
    is_live = slot_index[None, :] < count_row[:, None] * ROW_UNIT
    row_index = jnp.where(is_live, offsets[:, None] * ROW_UNIT + slot_index[None, :], 0).astype(jnp.int32)
    return (row_index, is_live)

def pick_labels(segment_row, row_index):
    return segment_row[row_index // ROW_UNIT]

def reference(residual_patch_matrix, transfer_tallies, picture_membership, premix_rescale_vector, triple_projection_matrix, per_head_sharpness, headmerge_projection_matrix, prefeed_rescale_vector, feedforward_expand_matrix, feedforward_contract_matrix):
    ff_local = FF // N_HEAD
    block_len = N_HEAD * CAP
    total_rows = N_HEAD * N_DP * CAP
    by_device = residual_patch_matrix.reshape(N_DP, N_HEAD, TOK_DEV, D)
    row_table, live_table = jax.vmap(send_rows)(transfer_tallies)
    label_table = jax.vmap(pick_labels)(picture_membership, row_table)
    label_table = jnp.where(live_table, label_table, -1).astype(jnp.int32)

    def per_group(destination):
        row_index = row_table[:, destination]
        is_live = live_table[:, destination]
        labels = label_table[:, destination]
        picked = by_device[jnp.arange(N_DP, dtype=jnp.int32)[:, None], :, row_index]
        picked = jnp.where(is_live[:, :, None, None], picked, jnp.zeros((), jnp.bfloat16))
        arrived = jnp.transpose(picked, (2, 0, 1, 3)).reshape(total_rows, D)
        normed = rms_scale(arrived.astype(jnp.float32), premix_rescale_vector).astype(jnp.bfloat16)
        qkv = shape_qkv(jnp.dot(normed, triple_projection_matrix, preferred_element_type=jnp.float32))
        qkv_parts = qkv.reshape(N_HEAD, N_DP, CAP, HEADS, 3, HEAD_DIM)
        qkv_parts = jnp.transpose(qkv_parts, (4, 1, 3, 0, 2, 5)).reshape(3, N_DP, HEADS, block_len, HEAD_DIM)
        token_labels = jnp.tile(labels, (1, N_HEAD))
        allowed = (token_labels[:, :, None] == token_labels[:, None, :]) & (token_labels[:, None, :] >= 0)
        pairwise_score_matrix = jnp.einsum('shid,shjd->shij', qkv_parts[0].astype(jnp.float32), qkv_parts[1].astype(jnp.float32))
        pairwise_score_matrix = pairwise_score_matrix * per_head_sharpness[None, :, None, None]
        pairwise_score_matrix = jnp.where(allowed[:, None], pairwise_score_matrix, jnp.float32(-1e+30))
        row_max = lax.optimization_barrier(jnp.max(pairwise_score_matrix, axis=-1, keepdims=True))
        weights_exp = jnp.exp(pairwise_score_matrix - row_max)
        probabilities = (weights_exp / lax.optimization_barrier(jnp.sum(weights_exp, axis=-1, keepdims=True))).astype(jnp.bfloat16)
        attended_heads = jnp.einsum('shij,shjd->shid', probabilities.astype(jnp.float32), qkv_parts[2].astype(jnp.float32))
        live_rows = token_labels >= 0
        attended_heads = jnp.where(live_rows[:, None, :, None], attended_heads, jnp.float32(0.0)).astype(jnp.bfloat16)
        attended_heads = attended_heads.reshape(N_DP, HEADS, N_HEAD, CAP, HEAD_DIM)
        attended_heads = jnp.transpose(attended_heads, (2, 0, 3, 1, 4)).reshape(total_rows, D)
        residual = arrived.astype(jnp.float32) + jnp.dot(attended_heads, headmerge_projection_matrix, preferred_element_type=jnp.float32)
        normed_mlp = rms_scale(residual, prefeed_rescale_vector).astype(jnp.bfloat16)
        hidden = jax.nn.gelu(jnp.dot(normed_mlp, feedforward_expand_matrix, preferred_element_type=jnp.float32), approximate=True)
        hidden = hidden.astype(jnp.bfloat16)

        def add_shard(running, shard_index):
            shard_cols = lax.dynamic_slice_in_dim(hidden, shard_index * ff_local, ff_local, 1)
            shard_weights = lax.dynamic_slice_in_dim(feedforward_contract_matrix, shard_index * ff_local, ff_local, 0)
            partial_term = jnp.dot(shard_cols, shard_weights, preferred_element_type=jnp.float32).astype(jnp.bfloat16)
            partial_term = lax.optimization_barrier(partial_term)
            return (running + partial_term.astype(jnp.float32), None)
        mlp_out, _ = lax.scan(add_shard, jnp.zeros((total_rows, D), jnp.float32), jnp.arange(N_HEAD, dtype=jnp.int32))
        return (residual + mlp_out).astype(jnp.bfloat16)
    outputs = lax.map(per_group, jnp.arange(N_DP, dtype=jnp.int32))
    return outputs.reshape(N_DP * total_rows, D)
```

```python
import jax
import jax.numpy as jnp
from jax import lax
from jax.sharding import Mesh
from jax.sharding import PartitionSpec as P

HEAD_DIM = 128
UNIT = 8
N_DP = 8
SIDE = 4
CAP = 24
EPS = 1e-06
DP = ("z", "c")


def ring(size, step):
    return [(i, (i + step) % size) for i in range(size)]


def rms_scale(values, gain_vector):
    mean_square = jnp.mean(values * values, axis=-1, keepdims=True)
    return values * lax.rsqrt(mean_square + EPS) * gain_vector


def unit_norm(values):
    mean_square = jnp.mean(values * values, axis=-1, keepdims=True)
    return values * lax.rsqrt(mean_square + EPS) * values.shape[-1] ** (-0.5)


def dot(a, b):
    return jnp.dot(a, b, preferred_element_type=jnp.float32)


def placement(tallies, membership, y):
    count = tallies[0]
    dest = jnp.arange(N_DP, dtype=jnp.int32)
    before = dest[None, :] < dest[:, None]
    offset = jnp.sum(jnp.where(before, count[None, :], 0), axis=1)
    ahead = (count[None, :] > count[:, None]) | ((count[None, :] == count[:, None]) & before)
    rank = jnp.sum(ahead.astype(jnp.int32), axis=1)
    first = rank < SIDE
    start = 4 * jnp.where(first, rank, 7 - rank) + jnp.where(first, 0, 4 - count)
    start = (start - 4 * y) % 16
    unit = jnp.arange(16, dtype=jnp.int32)
    inside = (unit[:, None] >= offset[None, :]) & (unit[:, None] < (offset + count)[None, :])
    place = jnp.sum(jnp.where(inside, (start - offset)[None, :], 0), axis=1) + unit
    key = jnp.sum(jnp.where(inside, dest[None, :] * 4, 0), axis=1) + membership[0]
    return count, start, place, key


def gather_halves(shard, axis, c):
    half = shard.shape[axis] // 2
    mine = lax.dynamic_slice_in_dim(shard, c * half, half, axis)
    parts = []
    for k in (1, 3, 2):
        got = lax.ppermute(mine, "y", ring(SIDE, k))
        parts.append((k, got))
    out = {}
    for k, got in parts:
        out[k] = (got, lax.ppermute(got, "c", ring(2, 1)))
    return out


def body(tokens, tallies, membership, gain1, wqkv, sharp, wmerge, gain2, w1, w2):
    z, c, y, x = (lax.axis_index(name) for name in ("z", "c", "y", "x"))
    count, start, place, key = placement(tallies, membership, y)
    row = jnp.arange(128, dtype=jnp.int32)
    target = jnp.repeat(place, UNIT) * UNIT + row % UNIT
    pick = (target[None, :] == row[:, None]).astype(jnp.bfloat16)
    picked = dot(pick, tokens).astype(jnp.bfloat16).reshape(SIDE, 32, -1)

    qkv_parts = gather_halves(wqkv, 0, c)
    w1_parts = gather_halves(w1, 1, c)
    w2_parts = gather_halves(w2, 0, c)
    sharps = [sharp] + [lax.ppermute(sharp, "y", ring(SIDE, k)) for k in (1, 2, 3)]

    column = jnp.concatenate(
        [picked[0]] + [lax.ppermute(picked[k], "y", ring(SIDE, k)) for k in (1, 2, 3)], 0
    )
    arrived = jnp.concatenate(
        [column] + [lax.ppermute(column, "x", ring(SIDE, m)) for m in (1, 2, 3)], 0
    )
    normed = rms_scale(arrived.astype(jnp.float32), gain1).astype(jnp.bfloat16)
    swapped = jnp.where(c == 0, normed, jnp.roll(normed, 1024, axis=1))

    quarter = jnp.arange(4, dtype=jnp.int32)
    key_of = jnp.sum(jnp.where(place[None, :] == quarter[:, None], key[None, :], 0), axis=1)
    keys = jnp.tile(jnp.repeat(key_of, UNIT), 16)
    allowed = keys[:, None] == keys[None, :]
    heads = []
    for k in range(SIDE):
        if k == 0:
            raw = dot(normed, wqkv)
        else:
            mine, other = qkv_parts[k]
            raw = dot(swapped[:, :1024], mine) + dot(swapped[:, 1024:], other)
        raw = raw.reshape(-1, 3, HEAD_DIM)
        q = unit_norm(raw[:, 0]).astype(jnp.bfloat16)
        kk = unit_norm(raw[:, 1]).astype(jnp.bfloat16)
        v = raw[:, 2].astype(jnp.bfloat16)
        score = dot(q, kk.T) * sharps[k][0]
        score = jnp.where(allowed, score, jnp.float32(-1e30))
        weights = jnp.exp(score - jnp.max(score, axis=-1, keepdims=True))
        p = (weights / jnp.sum(weights, axis=-1, keepdims=True)).astype(jnp.bfloat16)
        heads.append(dot(p, v).astype(jnp.bfloat16))
    mine = jnp.concatenate(heads, 1)

    merge_blocks = wmerge.reshape(SIDE, SIDE, HEAD_DIM, -1)
    order = jnp.arange(SIDE, dtype=jnp.int32)
    merge_blocks = merge_blocks[((y - order) % SIDE)[None, :], ((x - order) % SIDE)[:, None]]
    merge_blocks = merge_blocks.reshape(SIDE, SIDE * HEAD_DIM, -1)
    attended = [mine]
    for m in (1, 2, 3):
        got = lax.ppermute(mine, "x", ring(SIDE, m))
        attended.append(jnp.roll(got, 128 * m, axis=0))
    merged = dot(jnp.concatenate(attended, 1), merge_blocks.reshape(2048, -1))
    residual = arrived.astype(jnp.float32) + merged
    fed = rms_scale(residual, gain2).astype(jnp.bfloat16)

    total = None
    for k in range(SIDE):
        pairs = [(w1, w2)] if k == 0 else list(zip(w1_parts[k], w2_parts[k]))
        for up, down in pairs:
            hidden = jax.nn.gelu(dot(fed, up), approximate=True).astype(jnp.bfloat16)
            term = dot(hidden, down)
            total = term if total is None else total + term
    blocks = total.reshape(SIDE, 128, -1)
    done = residual[:128] + blocks[0]
    for j in (1, 2, 3):
        done = done + lax.ppermute(blocks[j].astype(jnp.bfloat16), "x", ring(SIDE, -j)).astype(
            jnp.float32
        )
    done = done.astype(jnp.bfloat16).reshape(SIDE, 32, -1)
    home = jnp.concatenate(
        [done[0]] + [lax.ppermute(done[k], "y", ring(SIDE, -k)) for k in (1, 2, 3)], 0
    )

    s = 2 * z + c
    turn = jnp.arange(N_DP, dtype=jnp.int32)
    dest = (s + turn) % N_DP
    slot = jnp.arange(CAP, dtype=jnp.int32)
    live = slot[None, :] < UNIT * count[dest][:, None]
    source = jnp.where(live, UNIT * start[dest][:, None] + slot[None, :], -1).reshape(-1)
    select = (source[:, None] == row[None, :]).astype(jnp.bfloat16)
    leaving = dot(select, home).astype(jnp.bfloat16).reshape(N_DP, CAP, -1)
    came = jnp.stack(
        [leaving[0]] + [lax.ppermute(leaving[m], DP, ring(N_DP, m)) for m in range(1, N_DP)], 0
    )
    return came[(s - turn) % N_DP].reshape(N_DP * CAP, -1)


def solution(mesh):
    grid = Mesh(mesh.devices.reshape(4, 2, 4, 4), ("z", "c", "y", "x"))
    head = ("y", "x")
    in_specs = (
        P(DP + head, None),
        P(DP, None),
        P(DP, None),
        P(),
        P(None, head),
        P(head),
        P(),
        P(),
        P(None, head),
        P(head, None),
    )
    return jax.shard_map(
        body, mesh=grid, in_specs=in_specs, out_specs=P(DP + head, None), check_vma=False
    )
```

```python
import functools

import jax
import jax.numpy as jnp
from jax import lax
from jax.experimental import pallas as pl
from jax.experimental.pallas import tpu as pltpu
from jax.sharding import Mesh
from jax.sharding import PartitionSpec as P

HEAD_DIM = 128
UNIT = 8
N_DP = 8
SIDE = 4
CAP = 24
EPS = 1e-06
DP = ("z", "c")
BF16 = jnp.bfloat16
F32 = jnp.float32
VMEM = pl.BlockSpec(memory_space=pltpu.VMEM)
SMEM = pl.BlockSpec(memory_space=pltpu.SMEM)
ANY = pl.BlockSpec(memory_space=pl.ANY)


def ring(size, step):
    return [(i, (i + step) % size) for i in range(size)]


def twin_ring():
    down = [(y, (y - 1) % SIDE) for y in range(SIDE)]
    up = [(SIDE + y, SIDE + (y + 1) % SIDE) for y in range(SIDE)]
    return down + up


def dot(a, b):
    return jnp.dot(a, b, preferred_element_type=F32)


def shape(dims, dtype=BF16):
    return jax.ShapeDtypeStruct(dims, dtype)


def call(kernel, outs, ins, scratch=(), vmem=100, flops=0, moved=0):
    return pl.pallas_call(
        kernel,
        out_shape=outs,
        in_specs=ins,
        out_specs=[VMEM] * len(outs),
        scratch_shapes=list(scratch),
        compiler_params=pltpu.CompilerParams(vmem_limit_bytes=vmem * 2**20 // 2),
        cost_estimate=pl.CostEstimate(flops=flops, bytes_accessed=moved, transcendentals=0),
    )


def placement(count_ref, y):
    count = [count_ref[0, d] for d in range(N_DP)]
    offset, start, running = [], [], jnp.int32(0)
    for d in range(N_DP):
        offset.append(running)
        running = running + count[d]
        rank = jnp.int32(0)
        for e in range(N_DP):
            if e != d:
                ahead = count[e] >= count[d] if e < d else count[e] > count[d]
                rank = rank + ahead.astype(jnp.int32)
        place = jnp.where(rank < SIDE, 4 * rank, 4 * (7 - rank) + 4 - count[d])
        start.append((place - 4 * y + 16) & 15)
    return count, offset, start


def spread(unit, count, offset, values):
    out = jnp.zeros_like(unit)
    for d in range(N_DP):
        inside = (unit >= offset[d]) & (unit < offset[d] + count[d])
        out = out + jnp.where(inside, values[d], 0)
    return out


def pick_kernel(where_ref, count_ref, tokens_ref, *outs):
    count, offset, start = placement(count_ref, where_ref[2])
    row = lax.broadcasted_iota(jnp.int32, (1, 128), 1)
    unit = row >> 3
    place = unit + spread(unit, count, offset, [s - o for s, o in zip(start, offset)])
    target = place * UNIT + (row & 7)
    pick = (target == lax.broadcasted_iota(jnp.int32, (128, 128), 0)).astype(F32).astype(BF16)
    for n in range(4):
        cols = pl.ds(512 * n, 512)
        picked = dot(pick, tokens_ref[:, cols]).astype(BF16)
        for k in range(SIDE):
            outs[k][:, cols] = picked[32 * k : 32 * k + 32]


def slice_kernel(where_ref, w1_ref, w2_ref, out_ref, sem):
    z = where_ref[0]
    copies = [
        pltpu.make_async_copy(
            w1_ref.at[pl.ds(pl.multiple_of(z * 512, 512), 512)], out_ref.at[pl.ds(0, 512)], sem.at[0]
        )
    ]
    for q in range(4):
        copies.append(
            pltpu.make_async_copy(
                w2_ref.at[pl.ds(pl.multiple_of(z * 128, 128), 128), pl.ds(512 * q, 512)],
                out_ref.at[pl.ds(512 + 128 * q, 128)],
                sem.at[1 + q],
            )
        )
    for copy in copies:
        copy.start()
    for copy in copies:
        copy.wait()


def half_kernel(where_ref, got_ref, out_ref):
    c = where_ref[1]
    out_ref[:256] = got_ref[pl.ds(pl.multiple_of(c * 256, 256), 256)]
    for q in range(4):
        out_ref[256 + 64 * q : 320 + 64 * q] = got_ref[
            pl.ds(pl.multiple_of(512 + 128 * q + 64 * c, 64), 64)
        ]


def pack_kernel(sharp_ref, wqkv_ref, out_ref, sem):
    copy = pltpu.make_async_copy(wqkv_ref, out_ref.at[pl.ds(0, 2048)], sem)
    copy.start()
    value = jnp.full((16, 384), sharp_ref[0], F32)
    high = value.astype(BF16).astype(F32)
    mid = (value - high).astype(BF16).astype(F32)
    low = value - high - mid
    lane = lax.broadcasted_iota(jnp.int32, (16, 384), 1)
    terms = jnp.where(lane == 0, high, jnp.where(lane == 1, mid, jnp.where(lane == 2, low, 0.0)))
    out_ref[2048:] = terms.astype(BF16)
    copy.wait()


def join_kernel(near_ref, far_ref, out_ref):
    out_ref[:1024] = near_ref[...]
    out_ref[1024:] = far_ref[...]


def far_kernel(where_ref, got_ref, out_ref):
    out_ref[:1024] = got_ref[pl.ds(pl.multiple_of(where_ref[1] * 1024, 1024), 1024)]
    out_ref[1024:] = got_ref[2048:]


def unit_norm(values):
    mean_square = jnp.mean(values * values, axis=-1, keepdims=True)
    return (values * lax.rsqrt(mean_square + EPS) * HEAD_DIM ** (-0.5)).astype(BF16)


def key_of_place(count_ref, member_ref, y):
    count, offset, start = placement(count_ref, y)
    row = (lax.broadcasted_iota(jnp.int32, (1, 512), 1) >> 3) & 3
    col = (lax.broadcasted_iota(jnp.int32, (512, 1), 0) >> 3) & 3
    key_row = jnp.zeros((1, 512), jnp.int32)
    key_col = jnp.zeros((512, 1), jnp.int32)
    for p in range(4):
        key = jnp.int32(0)
        for d in range(N_DP):
            inside = (start[d] <= p) & (p < start[d] + count[d])
            member = member_ref[0, jnp.where(inside, offset[d] + p - start[d], 0)]
            key = key + jnp.where(inside, d * 4 + member, 0)
        key_row = key_row + jnp.where(row == p, key, 0)
        key_col = key_col + jnp.where(col == p, key, 0)
    return key_col == key_row


def attend(raw, scale_row, allowed):
    q = unit_norm(raw[:, :128])
    k = unit_norm(raw[:, 128:256])
    v = raw[:, 256:].astype(BF16)
    score = lax.dot_general(q, k, (((1,), (1,)), ((), ())), preferred_element_type=F32)
    scale = jnp.sum(scale_row.astype(F32), axis=-1, keepdims=True)
    score = jnp.where(allowed, score * scale, -1e30)
    weights = jnp.exp(score - jnp.max(score, axis=-1, keepdims=True))
    p = (weights / jnp.sum(weights, axis=-1, keepdims=True)).astype(BF16)
    return dot(p, v).astype(BF16)


def norm_kernel(a0, a1, a2, a3, gain_ref, out_ref):
    for j, ref in enumerate((a0, a1, a2, a3)):
        values = ref[...].astype(F32)
        mean_square = jnp.mean(values * values, axis=-1, keepdims=True)
        out_ref[128 * j : 128 * j + 128] = (
            values * lax.rsqrt(mean_square + EPS) * gain_ref[...]
        ).astype(BF16)


def near_kernel(
    where_ref, count_ref, member_ref, xn, wq0, wq1, wq2, out_ref, w0, w1, w2, sem
):
    copies = [
        pltpu.make_async_copy(src, dst, sem.at[i])
        for i, (src, dst) in enumerate(((wq0, w0), (wq1, w1), (wq2, w2)))
    ]
    for copy in copies:
        copy.start()
    allowed = key_of_place(count_ref, member_ref, where_ref[2])
    for k, w in enumerate((w0, w1, w2)):
        copies[k].wait()
        raw = dot(xn[...], w[:2048])
        out_ref[:, 128 * k : 128 * k + 128] = attend(raw, w[2048:2049], allowed)


def far_attention_kernel(where_ref, count_ref, member_ref, xn, wqa, wqb, out_ref, w3, sem):
    c = where_ref[1]
    copies = [
        pltpu.make_async_copy(wqa, w3.at[c], sem.at[0]),
        pltpu.make_async_copy(wqb, w3.at[1 - c], sem.at[1]),
    ]
    for copy in copies:
        copy.start()
    allowed = key_of_place(count_ref, member_ref, where_ref[2])
    for copy in copies:
        copy.wait()
    raw = dot(xn[:, :1024], w3[0, :1024]) + dot(xn[:, 1024:], w3[1, :1024])
    out_ref[...] = attend(raw, w3[0, 1024:1025], allowed)


def merge_kernel(
    where_ref, a0, a1, a2, a3, o0, o1, o2, o3, f0, f1, f2, f3, gain_ref, wm, fed_ref, kept_ref,
    heads, total,
):
    c, y, x = where_ref[1], where_ref[2], where_ref[3]
    step = 1 - 2 * c
    source = [y, (y + step + 4) & 3, (y - step + 4) & 3, (y + 2) & 3]
    for m, (near, far) in enumerate(((o0, f0), (o1, f1), (o2, f2), (o3, f3))):
        for k in range(SIDE):
            head = source[k] * SIDE + ((x - m + 4) & 3)
            cols = pl.ds(pl.multiple_of(head * HEAD_DIM, HEAD_DIM), HEAD_DIM)
            for j in range(SIDE):
                theirs = slice(128 * ((j - m) % SIDE), 128 * ((j - m) % SIDE) + 128)
                block = far[theirs] if k == 3 else near[theirs, 128 * k : 128 * k + 128]
                heads[128 * j : 128 * j + 128, cols] = block
    squares = jnp.zeros((512, 1), F32)
    for n in range(4):
        cols = slice(512 * n, 512 * n + 512)
        part = dot(heads[...], wm[:, cols])
        arrived = jnp.concatenate([ref[:, cols] for ref in (a0, a1, a2, a3)], 0)
        part = part + arrived.astype(F32)
        squares = squares + jnp.sum(part * part, axis=-1, keepdims=True)
        total[:, cols] = part
    scale = lax.rsqrt(squares * (1.0 / 2048) + EPS)
    for n in range(4):
        cols = slice(512 * n, 512 * n + 512)
        fed_ref[:, cols] = (total[:, cols] * scale * gain_ref[:, cols]).astype(BF16)
    kept_ref[...] = total[:128]


def mlp_kernel(
    fed_ref, kept_ref, w1_ref, w2_ref, all_ref, own_ref, s1, s2, s3, w1, w2, hidden, sem
):
    copies = [
        [pltpu.make_async_copy(w1_ref, w1.at[0], sem.at[0])],
        [pltpu.make_async_copy(w2_ref, w2.at[pl.ds(0, 512)], sem.at[1])],
    ]
    for c in range(2):
        up, down = [], []
        for z in range(4):
            block = all_ref.at[2 * z + c]
            up.append(
                pltpu.make_async_copy(
                    block.at[pl.ds(0, 512)], w1.at[1 + c, pl.ds(512 * z, 512)], sem.at[2 + 2 * c]
                )
            )
            for q in range(4):
                down.append(
                    pltpu.make_async_copy(
                        block.at[pl.ds(512 + 128 * q, 128)],
                        w2.at[pl.ds(512 * (1 + c) + 128 * z, 128), pl.ds(512 * q, 512)],
                        sem.at[3 + 2 * c],
                    )
                )
        copies += [up, down]
    up, down = [], []
    for z in range(4):
        for c in range(2):
            block = all_ref.at[2 * z + c, pl.ds(1024, 512)]
            up.append(
                pltpu.make_async_copy(
                    block.at[pl.ds(0, 256)], w1.at[3, pl.ds(512 * z + 256 * c, 256)], sem.at[6]
                )
            )
            for q in range(4):
                down.append(
                    pltpu.make_async_copy(
                        block.at[pl.ds(256 + 64 * q, 64)],
                        w2.at[pl.ds(1536 + 128 * z + 64 * c, 64), pl.ds(512 * q, 512)],
                        sem.at[7],
                    )
                )
    copies += [up, down]
    for i in (0, 2, 4, 6, 1, 3, 5, 7):
        for copy in copies[i]:
            copy.start()
    for i in range(SIDE):
        for copy in copies[2 * i]:
            copy.wait()
        hidden[:, 512 * i : 512 * i + 512] = jax.nn.gelu(
            dot(fed_ref[...], w1[i]), approximate=True
        ).astype(BF16)
    for i in range(SIDE):
        for copy in copies[2 * i + 1]:
            copy.wait()
    for n in range(4):
        cols = slice(512 * n, 512 * n + 512)
        part = dot(hidden[...], w2[:, cols])
        own_ref[:, cols] = kept_ref[:, cols] + part[:128]
        for j, ref in enumerate((s1, s2, s3)):
            ref[:, cols] = part[128 * (j + 1) : 128 * (j + 2)].astype(BF16)


def sum_kernel(own_ref, r1, r2, r3, *outs):
    total = own_ref[...] + r1[...].astype(F32) + r2[...].astype(F32) + r3[...].astype(F32)
    total = total.astype(BF16)
    for k in range(SIDE):
        outs[k][...] = total[32 * k : 32 * k + 32]


def leave_kernel(where_ref, count_ref, h0, h1, h2, h3, stay_ref, cross_ref):
    z, c, y = where_ref[0], where_ref[1], where_ref[2]
    count, _, start = placement(count_ref, y)
    slot = lax.broadcasted_iota(jnp.int32, (192, 1), 0)
    block = slot // CAP
    inner = slot - block * CAP
    home = jnp.concatenate([h0[...], h1[...], h2[...], h3[...]], 0)
    target = jnp.full((192, 1), -1, jnp.int32)
    for d in range(N_DP):
        turn = ((d >> 1) - z + 4) & 3
        index = jnp.where((d & 1) == c, turn, 4 + turn)
        here = (block == index) & (inner < UNIT * count[d])
        target = jnp.where(here, UNIT * start[d] + inner, target)
    select = (target == lax.broadcasted_iota(jnp.int32, (192, 128), 1)).astype(F32).astype(BF16)
    moved = dot(select, home).astype(BF16).reshape(8, CAP, -1)
    stay_ref[...] = moved[:4]
    cross_ref[...] = moved[4:]


def pair_kernel(where_ref, stay_ref, cross_ref, *outs):
    c = where_ref[1]
    for m in range(SIDE):
        outs[m][c] = stay_ref[m]
        outs[m][1 - c] = cross_ref[m]


def order_kernel(where_ref, g0, g1, g2, g3, out_ref):
    for m, ref in enumerate((g0, g1, g2, g3)):
        out_ref[pl.ds(2 * ((where_ref[0] - m + 4) & 3), 2)] = ref[...]


def body(tokens, tallies, membership, gain1, wqkv, sharp, wmerge, gain2, w1, w2):
    z, c, y, x = (lax.axis_index(name) for name in ("z", "c", "y", "x"))
    where = jnp.stack([z, c, y, x]).astype(jnp.int32)
    gain1 = gain1[None]
    gain2 = gain2[None]
    cy = ("c", "y")

    blocks = call(pick_kernel, [shape((32, 2048))] * 4, [SMEM, SMEM, VMEM])(where, tallies, tokens)
    came = [blocks[0]] + [lax.ppermute(blocks[k], "y", ring(SIDE, k)) for k in (1, 2, 3)]
    w1_later, w2_later, _ = lax.optimization_barrier((w1, w2, blocks[1]))
    [mlp_slice] = call(
        slice_kernel,
        [shape((1024, 512))],
        [SMEM, ANY, ANY],
        [pltpu.SemaphoreType.DMA((5,))],
    )(where, w1_later, w2_later)
    near = lax.ppermute(mlp_slice, cy, twin_ring())
    [near_half] = call(half_kernel, [shape((512, 512))], [SMEM, VMEM])(where, near)
    far = lax.ppermute(near_half, cy, twin_ring())
    [both] = call(join_kernel, [shape((1536, 512))], [VMEM] * 2)(near, far)

    column = jnp.concatenate(came, 0)
    arrived = [column] + [lax.ppermute(column, "x", ring(SIDE, m)) for m in (1, 2, 3)]
    [packed] = call(
        pack_kernel,
        [shape((2064, 384))],
        [SMEM, ANY],
        [pltpu.SemaphoreType.DMA],
    )(sharp, lax.optimization_barrier((wqkv, column))[0])
    qkv_near = lax.ppermute(packed, cy, twin_ring())
    both_all = lax.all_gather(lax.optimization_barrier((both, column))[0], DP, axis=0, tiled=False)

    [normed] = call(norm_kernel, [shape((512, 2048))], [VMEM] * 5)(*arrived, gain1)
    qkv_near, normed = lax.optimization_barrier((qkv_near, normed))
    qkv_near2 = lax.ppermute(qkv_near, "c", ring(2, 1))
    [qkv_half] = call(far_kernel, [shape((1040, 384))], [SMEM, VMEM])(where, qkv_near)
    qkv_far = lax.ppermute(qkv_half, cy, twin_ring())
    qkv_far2 = lax.ppermute(qkv_far, "c", ring(2, 1))

    [mine] = call(
        near_kernel,
        [shape((512, 384))],
        [SMEM] * 3 + [VMEM] + [ANY] * 3,
        [pltpu.VMEM((2064, 384), BF16)] * 3 + [pltpu.SemaphoreType.DMA((3,))],
        flops=3 * 10**9,
        moved=10 * 2**20,
    )(where, tallies, membership, normed, packed, qkv_near, qkv_near2)
    [mine_far] = call(
        far_attention_kernel,
        [shape((512, 128))],
        [SMEM] * 3 + [VMEM] + [ANY] * 2,
        [pltpu.VMEM((2, 1040, 384), BF16), pltpu.SemaphoreType.DMA((2,))],
        flops=10**9,
        moved=4 * 2**20,
    )(where, tallies, membership, normed, qkv_far, qkv_far2)

    attended = [mine] + [lax.ppermute(mine, "x", ring(SIDE, m)) for m in (1, 2, 3)]
    attended += [mine_far] + [lax.ppermute(mine_far, "x", ring(SIDE, m)) for m in (1, 2, 3)]
    fed, kept = call(
        merge_kernel,
        [shape((512, 2048)), shape((128, 2048), F32)],
        [SMEM] + [VMEM] * 14,
        [pltpu.VMEM((512, 2048), BF16), pltpu.VMEM((512, 2048), F32)],
        flops=5 * 10**9,
        moved=14 * 2**20,
    )(where, *arrived, *attended, gain2, wmerge)

    own, s1, s2, s3 = call(
        mlp_kernel,
        [shape((128, 2048), F32)] + [shape((128, 2048))] * 3,
        [VMEM] * 2 + [ANY] * 3,
        [
            pltpu.VMEM((4, 2048, 512), BF16),
            pltpu.VMEM((2048, 2048), BF16),
            pltpu.VMEM((512, 2048), BF16),
            pltpu.SemaphoreType.DMA((8,)),
        ],
        flops=9 * 10**9,
        moved=20 * 2**20,
    )(fed, kept, w1, w2, both_all)
    sums = [lax.ppermute(s, "x", ring(SIDE, -j)) for j, s in ((1, s1), (2, s2), (3, s3))]
    done = call(sum_kernel, [shape((32, 2048))] * 4, [VMEM] * 4)(own, *sums)
    home = [done[0]] + [lax.ppermute(done[k], "y", ring(SIDE, -k)) for k in (1, 2, 3)]

    stay, cross = call(
        leave_kernel, [shape((4, CAP, 2048))] * 2, [SMEM, SMEM] + [VMEM] * 4
    )(where, tallies, *home)
    crossed = lax.ppermute(cross, "c", ring(2, 1))
    pairs = call(pair_kernel, [shape((2, CAP, 2048))] * 4, [SMEM] + [VMEM] * 2)(where, stay, crossed)
    got = [pairs[0]] + [lax.ppermute(pairs[m], "z", ring(SIDE, m)) for m in (1, 2, 3)]
    [out] = call(order_kernel, [shape((N_DP, CAP, 2048))], [SMEM] + [VMEM] * 4)(where, *got)
    return out.reshape(N_DP * CAP, -1)


def solution(mesh):
    grid = Mesh(mesh.devices.reshape(4, 2, 4, 4), ("z", "c", "y", "x"))
    head = ("y", "x")
    in_specs = (
        P(DP + head, None),
        P(DP, None),
        P(DP, None),
        P(),
        P(None, head),
        P(head),
        P(),
        P(),
        P(None, head),
        P(head, None),
    )
    return jax.shard_map(
        body, mesh=grid, in_specs=in_specs, out_specs=P(DP + head, None), check_vma=False
    )
```

```python
import functools

import jax
import jax.numpy as jnp
from jax import lax
from jax.experimental import pallas as pl
from jax.experimental.pallas import tpu as pltpu
from jax.sharding import Mesh
from jax.sharding import PartitionSpec as P

HEAD_DIM = 128
UNIT = 8
N_DP = 8
SIDE = 4
CAP = 24
EPS = 1e-06
DP = ("z", "c")
BF16 = jnp.bfloat16
F32 = jnp.float32
VMEM = pl.BlockSpec(memory_space=pltpu.VMEM)
SMEM = pl.BlockSpec(memory_space=pltpu.SMEM)
ANY = pl.BlockSpec(memory_space=pl.ANY)


def ring(size, step):
    return [(i, (i + step) % size) for i in range(size)]


def twin_ring():
    down = [(y, (y - 1) % SIDE) for y in range(SIDE)]
    up = [(SIDE + y, SIDE + (y + 1) % SIDE) for y in range(SIDE)]
    return down + up


def dot(a, b):
    return jnp.dot(a, b, preferred_element_type=F32)


def shape(dims, dtype=BF16):
    return jax.ShapeDtypeStruct(dims, dtype)


def call(kernel, outs, ins, scratch=(), vmem=100, flops=0, moved=0):
    return pl.pallas_call(
        kernel,
        out_shape=outs,
        in_specs=ins,
        out_specs=[VMEM] * len(outs),
        scratch_shapes=list(scratch),
        compiler_params=pltpu.CompilerParams(vmem_limit_bytes=vmem * 2**20 // 2),
        cost_estimate=pl.CostEstimate(flops=flops, bytes_accessed=moved, transcendentals=0),
    )


def placement(count_ref, y):
    count = [count_ref[0, d] for d in range(N_DP)]
    offset, start, running = [], [], jnp.int32(0)
    for d in range(N_DP):
        offset.append(running)
        running = running + count[d]
        rank = jnp.int32(0)
        for e in range(N_DP):
            if e != d:
                ahead = count[e] >= count[d] if e < d else count[e] > count[d]
                rank = rank + ahead.astype(jnp.int32)
        place = jnp.where(rank < SIDE, 4 * rank, 4 * (7 - rank) + 4 - count[d])
        start.append((place - 4 * y + 16) & 15)
    return count, offset, start


def spread(unit, count, offset, values):
    out = jnp.zeros_like(unit)
    for d in range(N_DP):
        inside = (unit >= offset[d]) & (unit < offset[d] + count[d])
        out = out + jnp.where(inside, values[d], 0)
    return out


def pick_kernel(where_ref, count_ref, tokens_ref, *outs):
    count, offset, start = placement(count_ref, where_ref[2])
    row = lax.broadcasted_iota(jnp.int32, (1, 128), 1)
    unit = row >> 3
    place = unit + spread(unit, count, offset, [s - o for s, o in zip(start, offset)])
    target = place * UNIT + (row & 7)
    pick = (target == lax.broadcasted_iota(jnp.int32, (128, 128), 0)).astype(F32).astype(BF16)
    for n in range(4):
        cols = pl.ds(512 * n, 512)
        picked = dot(pick, tokens_ref[:, cols]).astype(BF16)
        for k in range(SIDE):
            outs[k][:, cols] = picked[32 * k : 32 * k + 32]


def slice_kernel(where_ref, w1_ref, w2_ref, out_ref, sem):
    z = where_ref[0]
    copies = [
        pltpu.make_async_copy(
            w1_ref.at[pl.ds(pl.multiple_of(z * 512, 512), 512)], out_ref.at[pl.ds(0, 512)], sem.at[0]
        )
    ]
    for q in range(4):
        copies.append(
            pltpu.make_async_copy(
                w2_ref.at[pl.ds(pl.multiple_of(z * 128, 128), 128), pl.ds(512 * q, 512)],
                out_ref.at[pl.ds(512 + 128 * q, 128)],
                sem.at[1 + q],
            )
        )
    for copy in copies:
        copy.start()
    for copy in copies:
        copy.wait()


def half_kernel(where_ref, got_ref, out_ref):
    c = where_ref[1]
    out_ref[:256] = got_ref[pl.ds(pl.multiple_of(c * 256, 256), 256)]
    for q in range(4):
        out_ref[256 + 64 * q : 320 + 64 * q] = got_ref[
            pl.ds(pl.multiple_of(512 + 128 * q + 64 * c, 64), 64)
        ]


def pack_kernel(sharp_ref, wqkv_ref, out_ref, sem):
    copy = pltpu.make_async_copy(wqkv_ref, out_ref.at[pl.ds(0, 2048)], sem)
    copy.start()
    value = jnp.full((16, 384), sharp_ref[0], F32)
    high = value.astype(BF16).astype(F32)
    mid = (value - high).astype(BF16).astype(F32)
    low = value - high - mid
    lane = lax.broadcasted_iota(jnp.int32, (16, 384), 1)
    terms = jnp.where(lane == 0, high, jnp.where(lane == 1, mid, jnp.where(lane == 2, low, 0.0)))
    out_ref[2048:] = terms.astype(BF16)
    copy.wait()


def join_kernel(near_ref, far_ref, out_ref):
    out_ref[:1024] = near_ref[...]
    out_ref[1024:] = far_ref[...]


def far_kernel(where_ref, got_ref, out_ref):
    out_ref[:1024] = got_ref[pl.ds(pl.multiple_of(where_ref[1] * 1024, 1024), 1024)]
    out_ref[1024:] = got_ref[2048:]


def unit_norm(values):
    mean_square = jnp.mean(values * values, axis=-1, keepdims=True)
    return (values * lax.rsqrt(mean_square + EPS) * HEAD_DIM ** (-0.5)).astype(BF16)


def key_of_place(count_ref, member_ref, y):
    count, offset, start = placement(count_ref, y)
    row = (lax.broadcasted_iota(jnp.int32, (1, 512), 1) >> 3) & 3
    col = (lax.broadcasted_iota(jnp.int32, (512, 1), 0) >> 3) & 3
    key_row = jnp.zeros((1, 512), jnp.int32)
    key_col = jnp.zeros((512, 1), jnp.int32)
    for p in range(4):
        key = jnp.int32(0)
        for d in range(N_DP):
            inside = (start[d] <= p) & (p < start[d] + count[d])
            member = member_ref[0, jnp.where(inside, offset[d] + p - start[d], 0)]
            key = key + jnp.where(inside, d * 4 + member, 0)
        key_row = key_row + jnp.where(row == p, key, 0)
        key_col = key_col + jnp.where(col == p, key, 0)
    return key_col == key_row


def attend(raw, scale_row, allowed):
    q = unit_norm(raw[:, :128])
    k = unit_norm(raw[:, 128:256])
    v = raw[:, 256:].astype(BF16)
    score = lax.dot_general(q, k, (((1,), (1,)), ((), ())), preferred_element_type=F32)
    scale = jnp.sum(scale_row.astype(F32), axis=-1, keepdims=True)
    score = jnp.where(allowed, score * scale, -1e30)
    weights = jnp.exp(score - jnp.max(score, axis=-1, keepdims=True))
    p = (weights * (1.0 / jnp.sum(weights, axis=-1, keepdims=True))).astype(BF16)
    return dot(p, v).astype(BF16)


def norm_kernel(a0, a1, a2, a3, gain_ref, out_ref):
    for j, ref in enumerate((a0, a1, a2, a3)):
        values = ref[...].astype(F32)
        mean_square = jnp.mean(values * values, axis=-1, keepdims=True)
        out_ref[128 * j : 128 * j + 128] = (
            values * lax.rsqrt(mean_square + EPS) * gain_ref[...]
        ).astype(BF16)


def near_kernel(where_ref, count_ref, member_ref, xn, wq0, wq1, out_ref, w0, w1, sem):
    copies = [
        pltpu.make_async_copy(src, dst, sem.at[i])
        for i, (src, dst) in enumerate(((wq0, w0), (wq1, w1)))
    ]
    for copy in copies:
        copy.start()
    allowed = key_of_place(count_ref, member_ref, where_ref[2])
    for k, w in enumerate((w0, w1)):
        copies[k].wait()
        raw = dot(xn[...], w[:2048])
        out_ref[:, 128 * k : 128 * k + 128] = attend(raw, w[2048:2049], allowed)


def far_attention_kernel(where_ref, count_ref, member_ref, xn, wq2, wqa, wqb, out_ref, w2, w3, sem):
    c = where_ref[1]
    copies = [
        pltpu.make_async_copy(wq2, w2, sem.at[0]),
        pltpu.make_async_copy(wqa, w3.at[c], sem.at[1]),
        pltpu.make_async_copy(wqb, w3.at[1 - c], sem.at[2]),
    ]
    for copy in copies:
        copy.start()
    allowed = key_of_place(count_ref, member_ref, where_ref[2])
    copies[0].wait()
    out_ref[:, :128] = attend(dot(xn[...], w2[:2048]), w2[2048:2049], allowed)
    copies[1].wait()
    copies[2].wait()
    raw = dot(xn[:, :1024], w3[0, :1024]) + dot(xn[:, 1024:], w3[1, :1024])
    out_ref[:, 128:] = attend(raw, w3[0, 1024:1025], allowed)


def merge_kernel(
    where_ref, a0, a1, a2, a3, o0, o1, o2, o3, f0, f1, f2, f3, gain_ref, wm, fed_ref, kept_ref,
    heads, total,
):
    c, y, x = where_ref[1], where_ref[2], where_ref[3]
    step = 1 - 2 * c
    source = [y, (y + step + 4) & 3, (y - step + 4) & 3, (y + 2) & 3]
    for m, (near, far) in enumerate(((o0, f0), (o1, f1), (o2, f2), (o3, f3))):
        for k in range(SIDE):
            head = source[k] * SIDE + ((x - m + 4) & 3)
            cols = pl.ds(pl.multiple_of(head * HEAD_DIM, HEAD_DIM), HEAD_DIM)
            for j in range(SIDE):
                theirs = slice(128 * ((j - m) % SIDE), 128 * ((j - m) % SIDE) + 128)
                block = (near, far)[k // 2][theirs, 128 * (k % 2) : 128 * (k % 2) + 128]
                heads[128 * j : 128 * j + 128, cols] = block
    squares = jnp.zeros((512, 1), F32)
    for n in range(4):
        cols = slice(512 * n, 512 * n + 512)
        part = dot(heads[...], wm[:, cols])
        arrived = jnp.concatenate([ref[:, cols] for ref in (a0, a1, a2, a3)], 0)
        part = part + arrived.astype(F32)
        squares = squares + jnp.sum(part * part, axis=-1, keepdims=True)
        total[:, cols] = part
    scale = lax.rsqrt(squares * (1.0 / 2048) + EPS)
    for n in range(4):
        cols = slice(512 * n, 512 * n + 512)
        fed_ref[:, cols] = (total[:, cols] * scale * gain_ref[:, cols]).astype(BF16)
    kept_ref[...] = total[:128]


def mlp_kernel(
    where_ref, fed_ref, kept_ref, w1_ref, w2_ref, all_ref, out_ref, w1, w2, hidden, sem
):
    copies = [
        [pltpu.make_async_copy(w1_ref, w1.at[0], sem.at[0])],
        [pltpu.make_async_copy(w2_ref, w2.at[pl.ds(0, 512)], sem.at[1])],
    ]
    for c in range(2):
        up, down = [], []
        for z in range(4):
            block = all_ref.at[2 * z + c]
            up.append(
                pltpu.make_async_copy(
                    block.at[pl.ds(0, 512)], w1.at[1 + c, pl.ds(512 * z, 512)], sem.at[2 + 2 * c]
                )
            )
            for q in range(4):
                down.append(
                    pltpu.make_async_copy(
                        block.at[pl.ds(512 + 128 * q, 128)],
                        w2.at[pl.ds(512 * (1 + c) + 128 * z, 128), pl.ds(512 * q, 512)],
                        sem.at[3 + 2 * c],
                    )
                )
        copies += [up, down]
    up, down = [], []
    for z in range(4):
        for c in range(2):
            block = all_ref.at[2 * z + c, pl.ds(1024, 512)]
            up.append(
                pltpu.make_async_copy(
                    block.at[pl.ds(0, 256)], w1.at[3, pl.ds(512 * z + 256 * c, 256)], sem.at[6]
                )
            )
            for q in range(4):
                down.append(
                    pltpu.make_async_copy(
                        block.at[pl.ds(256 + 64 * q, 64)],
                        w2.at[pl.ds(1536 + 128 * z + 64 * c, 64), pl.ds(512 * q, 512)],
                        sem.at[7],
                    )
                )
    copies += [up, down]
    for i in (0, 2, 4, 6, 1, 3, 5, 7):
        for copy in copies[i]:
            copy.start()
    for i in range(SIDE):
        for copy in copies[2 * i]:
            copy.wait()
        hidden[:, 512 * i : 512 * i + 512] = jax.nn.gelu(
            dot(fed_ref[...], w1[i]), approximate=True
        ).astype(BF16)
    for i in range(SIDE):
        for copy in copies[2 * i + 1]:
            copy.wait()
    for n in range(4):
        cols = slice(512 * n, 512 * n + 512)
        part = dot(hidden[...], w2[:, cols])
        for j in range(SIDE):
            for k in range(SIDE):
                rows = slice(128 * j + 32 * k, 128 * j + 32 * k + 32)
                home = ((where_ref[2] - k + 4) & 3) * SIDE + ((where_ref[3] - j + 4) & 3)
                block = part[rows]
                if j == 0:
                    block = block + kept_ref[rows, cols]
                out_ref[home, :, cols] = block.astype(BF16)


def leave_kernel(where_ref, count_ref, parts_ref, stay_ref, cross_ref):
    z, c = where_ref[0], where_ref[1]
    count, _, start = placement(count_ref, 0)
    slot = lax.broadcasted_iota(jnp.int32, (192, 1), 0)
    block = slot // CAP
    inner = slot - block * CAP
    rows = []
    for y in range(SIDE):
        total = parts_ref[4 * y].astype(F32)
        for x in range(1, SIDE):
            total = total + parts_ref[4 * y + x].astype(F32)
        rows.append(total.astype(BF16))
    home = jnp.concatenate(rows, 0)
    target = jnp.full((192, 1), -1, jnp.int32)
    for d in range(N_DP):
        turn = ((d >> 1) - z + 4) & 3
        index = jnp.where((d & 1) == c, turn, 4 + turn)
        here = (block == index) & (inner < UNIT * count[d])
        target = jnp.where(here, UNIT * start[d] + inner, target)
    select = (target == lax.broadcasted_iota(jnp.int32, (192, 128), 1)).astype(F32).astype(BF16)
    moved = dot(select, home).astype(BF16).reshape(8, CAP, -1)
    stay_ref[...] = moved[:4]
    cross_ref[...] = moved[4:]


def pair_kernel(where_ref, stay_ref, cross_ref, *outs):
    c = where_ref[1]
    for m in range(SIDE):
        outs[m][c] = stay_ref[m]
        outs[m][1 - c] = cross_ref[m]


def order_kernel(where_ref, g0, g1, g2, g3, out_ref):
    for m, ref in enumerate((g0, g1, g2, g3)):
        out_ref[pl.ds(2 * ((where_ref[0] - m + 4) & 3), 2)] = ref[...]


def body(tokens, tallies, membership, gain1, wqkv, sharp, wmerge, gain2, w1, w2):
    z, c, y, x = (lax.axis_index(name) for name in ("z", "c", "y", "x"))
    where = jnp.stack([z, c, y, x]).astype(jnp.int32)
    gain1 = gain1[None]
    gain2 = gain2[None]
    cy = ("c", "y")

    blocks = call(
        pick_kernel, [shape((32, 2048))] * 4, [SMEM, SMEM, VMEM], flops=10 * 10**9
    )(where, tallies, tokens)
    came = [blocks[0]] + [lax.ppermute(blocks[k], "y", ring(SIDE, k)) for k in (1, 2, 3)]
    w1_later, w2_later, _ = lax.optimization_barrier((w1, w2, blocks[1]))
    [mlp_slice] = call(
        slice_kernel,
        [shape((1024, 512))],
        [SMEM, ANY, ANY],
        [pltpu.SemaphoreType.DMA((5,))],
    )(where, w1_later, w2_later)
    near = lax.ppermute(mlp_slice, cy, twin_ring())
    column = jnp.concatenate(came, 0)
    near, column = lax.optimization_barrier((near, column))
    [near_half] = call(half_kernel, [shape((512, 512))], [SMEM, VMEM])(where, near)
    far = lax.ppermute(near_half, cy, twin_ring())
    [both] = call(join_kernel, [shape((1536, 512))], [VMEM] * 2)(near, far)

    arrived = [column] + [lax.ppermute(column, "x", ring(SIDE, m)) for m in (1, 2, 3)]
    [packed] = call(
        pack_kernel,
        [shape((2064, 384))],
        [SMEM, ANY],
        [pltpu.SemaphoreType.DMA],
    )(sharp, lax.optimization_barrier((wqkv, column))[0])
    qkv_near = lax.ppermute(packed, cy, twin_ring())
    both_all = lax.all_gather(both, DP, axis=0, tiled=False)

    [normed] = call(norm_kernel, [shape((512, 2048))], [VMEM] * 5, flops=25 * 10**9)(
        *arrived, gain1
    )
    qkv_near, normed = lax.optimization_barrier((qkv_near, normed))
    qkv_near2 = lax.ppermute(qkv_near, "c", ring(2, 1))
    [qkv_half] = call(far_kernel, [shape((1040, 384))], [SMEM, VMEM])(where, qkv_near)
    qkv_far = lax.ppermute(qkv_half, cy, twin_ring())

    [mine] = call(
        near_kernel,
        [shape((512, 256))],
        [SMEM] * 3 + [VMEM] + [ANY] * 2,
        [pltpu.VMEM((2064, 384), BF16)] * 2 + [pltpu.SemaphoreType.DMA((2,))],
        flops=2 * 10**9,
        moved=8 * 2**20,
    )(where, tallies, membership, normed, packed, qkv_near)
    qkv_far, mine = lax.optimization_barrier((qkv_far, mine))
    qkv_far2 = lax.ppermute(qkv_far, "c", ring(2, 1))
    [mine_far] = call(
        far_attention_kernel,
        [shape((512, 256))],
        [SMEM] * 3 + [VMEM] + [ANY] * 3,
        [
            pltpu.VMEM((2064, 384), BF16),
            pltpu.VMEM((2, 1040, 384), BF16),
            pltpu.SemaphoreType.DMA((3,)),
        ],
        flops=2 * 10**9,
        moved=8 * 2**20,
    )(where, tallies, membership, normed, qkv_near2, qkv_far, qkv_far2)

    attended = [mine] + [lax.ppermute(mine, "x", ring(SIDE, m)) for m in (1, 2, 3)]
    attended += [mine_far] + [lax.ppermute(mine_far, "x", ring(SIDE, m)) for m in (1, 2, 3)]
    fed, kept = call(
        merge_kernel,
        [shape((512, 2048)), shape((128, 2048), F32)],
        [SMEM] + [VMEM] * 14,
        [pltpu.VMEM((512, 2048), BF16), pltpu.VMEM((512, 2048), F32)],
        flops=25 * 10**9,
        moved=14 * 2**20,
    )(where, *arrived, *attended, gain2, wmerge)

    [parts] = call(
        mlp_kernel,
        [shape((16, 32, 2048))],
        [SMEM] + [VMEM] * 2 + [ANY] * 3,
        [
            pltpu.VMEM((4, 2048, 512), BF16),
            pltpu.VMEM((2048, 2048), BF16),
            pltpu.VMEM((512, 2048), BF16),
            pltpu.SemaphoreType.DMA((8,)),
        ],
        flops=9 * 10**9,
        moved=20 * 2**20,
    )(where, fed, kept, w1, w2, both_all)
    parts = lax.all_to_all(parts, ("y", "x"), 0, 0, tiled=True)
    stay, cross = call(leave_kernel, [shape((4, CAP, 2048))] * 2, [SMEM, SMEM, VMEM])(
        where, tallies, parts
    )
    crossed = lax.ppermute(cross, "c", ring(2, 1))
    pairs = call(pair_kernel, [shape((2, CAP, 2048))] * 4, [SMEM] + [VMEM] * 2)(where, stay, crossed)
    got = [pairs[0]] + [lax.ppermute(pairs[m], "z", ring(SIDE, m)) for m in (1, 2, 3)]
    [out] = call(order_kernel, [shape((N_DP, CAP, 2048))], [SMEM] + [VMEM] * 4)(where, *got)
    return out.reshape(N_DP * CAP, -1)


def solution(mesh):
    grid = Mesh(mesh.devices.reshape(4, 2, 4, 4), ("z", "c", "y", "x"))
    head = ("y", "x")
    in_specs = (
        P(DP + head, None),
        P(DP, None),
        P(DP, None),
        P(),
        P(None, head),
        P(head),
        P(),
        P(),
        P(None, head),
        P(head, None),
    )
    return jax.shard_map(
        body, mesh=grid, in_specs=in_specs, out_specs=P(DP + head, None), check_vma=False
    )
```

```python
import functools

import jax
import jax.numpy as jnp
from jax import lax
from jax.experimental import pallas as pl
from jax.experimental.pallas import tpu as pltpu
from jax.sharding import Mesh
from jax.sharding import PartitionSpec as P

HEAD_DIM = 128
UNIT = 8
N_DP = 8
SIDE = 4
CAP = 24
EPS = 1e-06
DP = ("z", "c")
BF16 = jnp.bfloat16
F32 = jnp.float32
VMEM = pl.BlockSpec(memory_space=pltpu.VMEM)
SMEM = pl.BlockSpec(memory_space=pltpu.SMEM)
ANY = pl.BlockSpec(memory_space=pl.ANY)


def ring(size, step):
    return [(i, (i + step) % size) for i in range(size)]


def twin_ring():
    down = [(y, (y - 1) % SIDE) for y in range(SIDE)]
    up = [(SIDE + y, SIDE + (y + 1) % SIDE) for y in range(SIDE)]
    return down + up


def dot(a, b):
    return jnp.dot(a, b, preferred_element_type=F32)


def shape(dims, dtype=BF16):
    return jax.ShapeDtypeStruct(dims, dtype)


def call(kernel, outs, ins, scratch=(), vmem=6, flops=0, moved=0):
    return pl.pallas_call(
        kernel,
        out_shape=outs,
        in_specs=ins,
        out_specs=[VMEM] * len(outs),
        scratch_shapes=list(scratch),
        compiler_params=pltpu.CompilerParams(vmem_limit_bytes=vmem * 2**20),
        cost_estimate=pl.CostEstimate(flops=flops, bytes_accessed=moved, transcendentals=0),
    )


def placement(count_ref, y):
    count = [count_ref[0, d] for d in range(N_DP)]
    offset, start, running = [], [], jnp.int32(0)
    for d in range(N_DP):
        offset.append(running)
        running = running + count[d]
        rank = jnp.int32(0)
        for e in range(N_DP):
            if e != d:
                ahead = count[e] >= count[d] if e < d else count[e] > count[d]
                rank = rank + ahead.astype(jnp.int32)
        place = jnp.where(rank < SIDE, 4 * rank, 4 * (7 - rank) + 4 - count[d])
        start.append((place - 4 * y + 16) & 15)
    return count, offset, start


def spread(unit, count, offset, values):
    out = jnp.zeros_like(unit)
    for d in range(N_DP):
        inside = (unit >= offset[d]) & (unit < offset[d] + count[d])
        out = out + jnp.where(inside, values[d], 0)
    return out


def pick_kernel(where_ref, count_ref, tokens_ref, *outs):
    count, offset, start = placement(count_ref, where_ref[2])
    row = lax.broadcasted_iota(jnp.int32, (1, 128), 1)
    unit = row >> 3
    place = unit + spread(unit, count, offset, [s - o for s, o in zip(start, offset)])
    target = place * UNIT + (row & 7)
    pick = (target == lax.broadcasted_iota(jnp.int32, (128, 128), 0)).astype(F32).astype(BF16)
    for n in range(4):
        cols = pl.ds(512 * n, 512)
        picked = dot(pick, tokens_ref[:, cols]).astype(BF16)
        for k in range(SIDE):
            outs[k][:, cols] = picked[32 * k : 32 * k + 32]


def slice_kernel(where_ref, w1_ref, w2_ref, out_ref, sem):
    z = where_ref[0]
    copies = [
        pltpu.make_async_copy(
            w1_ref.at[pl.ds(pl.multiple_of(z * 512, 512), 512)], out_ref.at[pl.ds(0, 512)], sem.at[0]
        )
    ]
    for q in range(4):
        copies.append(
            pltpu.make_async_copy(
                w2_ref.at[pl.ds(pl.multiple_of(z * 128, 128), 128), pl.ds(512 * q, 512)],
                out_ref.at[pl.ds(512 + 128 * q, 128)],
                sem.at[1 + q],
            )
        )
    for copy in copies:
        copy.start()
    for copy in copies:
        copy.wait()


def half_kernel(where_ref, got_ref, out_ref):
    c = where_ref[1]
    out_ref[:256] = got_ref[pl.ds(pl.multiple_of(c * 256, 256), 256)]
    for q in range(4):
        out_ref[256 + 64 * q : 320 + 64 * q] = got_ref[
            pl.ds(pl.multiple_of(512 + 128 * q + 64 * c, 64), 64)
        ]


def pack_kernel(sharp_ref, wqkv_ref, out_ref, sem):
    copy = pltpu.make_async_copy(wqkv_ref, out_ref.at[pl.ds(0, 2048)], sem)
    copy.start()
    value = jnp.full((16, 384), sharp_ref[0], F32)
    high = value.astype(BF16).astype(F32)
    mid = (value - high).astype(BF16).astype(F32)
    low = value - high - mid
    lane = lax.broadcasted_iota(jnp.int32, (16, 384), 1)
    terms = jnp.where(lane == 0, high, jnp.where(lane == 1, mid, jnp.where(lane == 2, low, 0.0)))
    out_ref[2048:] = terms.astype(BF16)
    copy.wait()


def far_kernel(where_ref, got_ref, out_ref):
    out_ref[:1024] = got_ref[pl.ds(pl.multiple_of(where_ref[1] * 1024, 1024), 1024)]
    out_ref[1024:] = got_ref[2048:]


def unit_norm(values):
    mean_square = jnp.mean(values * values, axis=-1, keepdims=True)
    return (values * lax.rsqrt(mean_square + EPS) * HEAD_DIM ** (-0.5)).astype(BF16)


def key_of_place(count_ref, member_ref, y):
    count, offset, start = placement(count_ref, y)
    row = (lax.broadcasted_iota(jnp.int32, (1, 512), 1) >> 3) & 3
    col = (lax.broadcasted_iota(jnp.int32, (512, 1), 0) >> 3) & 3
    key_row = jnp.zeros((1, 512), jnp.int32)
    key_col = jnp.zeros((512, 1), jnp.int32)
    for p in range(4):
        key = jnp.int32(0)
        for d in range(N_DP):
            inside = (start[d] <= p) & (p < start[d] + count[d])
            member = member_ref[0, jnp.where(inside, offset[d] + p - start[d], 0)]
            key = key + jnp.where(inside, d * 4 + member, 0)
        key_row = key_row + jnp.where(row == p, key, 0)
        key_col = key_col + jnp.where(col == p, key, 0)
    return key_col == key_row


def attend(raw, scale_row, allowed):
    q = unit_norm(raw[:, :128])
    k = unit_norm(raw[:, 128:256])
    v = raw[:, 256:].astype(BF16)
    score = lax.dot_general(q, k, (((1,), (1,)), ((), ())), preferred_element_type=F32)
    scale = jnp.sum(scale_row.astype(F32), axis=-1, keepdims=True)
    score = jnp.where(allowed, score * scale, -1e30)
    weights = jnp.exp(score - jnp.max(score, axis=-1, keepdims=True))
    p = (weights * (1.0 / jnp.sum(weights, axis=-1, keepdims=True))).astype(BF16)
    return dot(p, v).astype(BF16)


def norm_kernel(a0, a1, a2, a3, gain_ref, out_ref, kept_ref, sem):
    copies = [
        pltpu.make_async_copy(ref, kept_ref.at[pl.ds(128 * j, 128)], sem.at[j])
        for j, ref in enumerate((a0, a1, a2, a3))
    ]
    for copy in copies:
        copy.start()
    for j, copy in enumerate(copies):
        rows = slice(128 * j, 128 * j + 128)
        copy.wait()
        values = kept_ref[rows].astype(F32)
        mean_square = jnp.mean(values * values, axis=-1, keepdims=True)
        out_ref[rows] = (values * lax.rsqrt(mean_square + EPS) * gain_ref[...]).astype(BF16)


def near_kernel(where_ref, count_ref, member_ref, xn, wq0, wq1, out_ref, w0, w1, sem):
    copies = [
        pltpu.make_async_copy(src, dst, sem.at[i])
        for i, (src, dst) in enumerate(((wq0, w0), (wq1, w1)))
    ]
    for copy in copies:
        copy.start()
    allowed = key_of_place(count_ref, member_ref, where_ref[2])
    for k, w in enumerate((w0, w1)):
        copies[k].wait()
        raw = dot(xn[...], w[:2048])
        out_ref[:, 128 * k : 128 * k + 128] = attend(raw, w[2048:2049], allowed)


def far_attention_kernel(where_ref, count_ref, member_ref, xn, wq2, wqa, wqb, out_ref, w2, w3, sem):
    c = where_ref[1]
    copies = [
        pltpu.make_async_copy(wq2, w2, sem.at[0]),
        pltpu.make_async_copy(wqa, w3.at[c], sem.at[1]),
        pltpu.make_async_copy(wqb, w3.at[1 - c], sem.at[2]),
    ]
    for copy in copies:
        copy.start()
    allowed = key_of_place(count_ref, member_ref, where_ref[2])
    copies[0].wait()
    out_ref[:, :128] = attend(dot(xn[...], w2[:2048]), w2[2048:2049], allowed)
    copies[1].wait()
    copies[2].wait()
    raw = dot(xn[:, :1024], w3[0, :1024]) + dot(xn[:, 1024:], w3[1, :1024])
    out_ref[:, 128:] = attend(raw, w3[0, 1024:1025], allowed)


def merge_part(where_ref, pair, refs, wm_ref, wm, heads, sem):
    c, y, x = where_ref[1], where_ref[2], where_ref[3]
    step = 1 - 2 * c
    source = ([y, (y + step + 4) & 3], [(y - step + 4) & 3, (y + 2) & 3])[pair]
    copies = []
    for m in range(SIDE):
        for k in range(2):
            head = source[k] * SIDE + ((x - m + 4) & 3)
            copies.append(
                pltpu.make_async_copy(
                    wm_ref.at[pl.ds(pl.multiple_of(head * HEAD_DIM, HEAD_DIM), HEAD_DIM)],
                    wm.at[pl.ds(256 * m + HEAD_DIM * k, HEAD_DIM)],
                    sem.at[2 * m + k],
                )
            )
    for copy in copies:
        copy.start()
    for m, ref in enumerate(refs):
        for j in range(SIDE):
            theirs = 128 * ((j - m) % SIDE)
            heads[128 * j : 128 * j + 128, 256 * m : 256 * m + 256] = ref[theirs : theirs + 128]
    for copy in copies:
        copy.wait()


def merge_first_kernel(where_ref, o0, o1, o2, o3, rows_ref, wm_ref, out_ref, wm, heads, rows, sem):
    carried = pltpu.make_async_copy(rows_ref, rows, sem.at[8])
    carried.start()
    merge_part(where_ref, 0, (o0, o1, o2, o3), wm_ref, wm, heads, sem)
    carried.wait()
    for n in range(4):
        cols = slice(512 * n, 512 * n + 512)
        out_ref[:, cols] = dot(heads[...], wm[:, cols]) + rows[:, cols].astype(F32)


def merge_kernel(
    where_ref, f0, f1, f2, f3, gain_ref, part_ref, wm_ref, fed_ref, kept_ref, wm, heads, total, sem
):
    carried = pltpu.make_async_copy(part_ref, total, sem.at[8])
    carried.start()
    merge_part(where_ref, 1, (f0, f1, f2, f3), wm_ref, wm, heads, sem)
    carried.wait()
    squares = jnp.zeros((512, 1), F32)
    for n in range(4):
        cols = slice(512 * n, 512 * n + 512)
        part = dot(heads[...], wm[:, cols]) + total[:, cols]
        squares = squares + jnp.sum(part * part, axis=-1, keepdims=True)
        total[:, cols] = part
    scale = lax.rsqrt(squares * (1.0 / 2048) + EPS)
    for n in range(4):
        cols = slice(512 * n, 512 * n + 512)
        fed_ref[:, cols] = (total[:, cols] * scale * gain_ref[:, cols]).astype(BF16)
    kept_ref[...] = total[:128]


def near_mlp_kernel(fed_ref, w1_ref, all_ref, out_ref, w1, sem):
    copies = [[pltpu.make_async_copy(w1_ref, w1.at[0], sem.at[0])]]
    for c in range(2):
        copies.append(
            [
                pltpu.make_async_copy(
                    all_ref.at[2 * z + c, pl.ds(0, 512)],
                    w1.at[1 + c, pl.ds(512 * z, 512)],
                    sem.at[1 + c],
                )
                for z in range(4)
            ]
        )
    for group in copies:
        for copy in group:
            copy.start()
    for i in range(3):
        for copy in copies[i]:
            copy.wait()
        out_ref[:, 512 * i : 512 * i + 512] = jax.nn.gelu(
            dot(fed_ref[...], w1[i]), approximate=True
        ).astype(BF16)


def far_mlp_kernel(
    where_ref, fed_ref, kept_ref, hidden_ref, w2_ref, near_ref, far_ref, out_ref,
    w1, w2, hidden, kept, sem,
):
    ups, downs = [], []
    for z in range(4):
        for c in range(2):
            block = far_ref.at[2 * z + c]
            ups.append(
                pltpu.make_async_copy(
                    block.at[pl.ds(0, 256)], w1.at[pl.ds(512 * z + 256 * c, 256)], sem.at[0]
                )
            )
    carried = [
        pltpu.make_async_copy(hidden_ref, hidden.at[:, pl.ds(0, 1536)], sem.at[1]),
        pltpu.make_async_copy(kept_ref, kept, sem.at[1]),
    ]
    for n in range(4):
        cols = pl.ds(512 * n, 512)
        down = [pltpu.make_async_copy(w2_ref.at[:, cols], w2.at[pl.ds(0, 512), cols], sem.at[2 + n])]
        for c in range(2):
            for z in range(4):
                down.append(
                    pltpu.make_async_copy(
                        near_ref.at[2 * z + c, pl.ds(512 + 128 * n, 128)],
                        w2.at[pl.ds(512 * (1 + c) + 128 * z, 128), cols],
                        sem.at[2 + n],
                    )
                )
                down.append(
                    pltpu.make_async_copy(
                        far_ref.at[2 * z + c, pl.ds(256 + 64 * n, 64)],
                        w2.at[pl.ds(1536 + 128 * z + 64 * c, 64), cols],
                        sem.at[2 + n],
                    )
                )
        downs.append(down)
    for copies in [ups, carried, *downs]:
        for copy in copies:
            copy.start()
    for copy in ups:
        copy.wait()
    hidden[:, 1536:] = jax.nn.gelu(dot(fed_ref[...], w1[...]), approximate=True).astype(BF16)
    for copy in carried:
        copy.wait()
    for n in range(4):
        cols = slice(512 * n, 512 * n + 512)
        for copy in downs[n]:
            copy.wait()
        part = dot(hidden[...], w2[:, cols])
        for j in range(SIDE):
            for k in range(SIDE):
                rows = slice(128 * j + 32 * k, 128 * j + 32 * k + 32)
                home = ((where_ref[2] - k + 4) & 3) * SIDE + ((where_ref[3] - j + 4) & 3)
                block = part[rows]
                if j == 0:
                    block = block + kept[rows, cols]
                out_ref[home, :, cols] = block.astype(BF16)


def leave_kernel(where_ref, count_ref, parts_ref, *outs):
    group = 2 * where_ref[0] + where_ref[1]
    count, _, start = placement(count_ref, 0)
    slot = lax.broadcasted_iota(jnp.int32, (192, 1), 0)
    block = slot // CAP
    inner = slot - block * CAP
    rows = []
    for y in range(SIDE):
        total = parts_ref[4 * y].astype(F32)
        for x in range(1, SIDE):
            total = total + parts_ref[4 * y + x].astype(F32)
        rows.append(total.astype(BF16))
    home = jnp.concatenate(rows, 0)
    target = jnp.full((192, 1), -1, jnp.int32)
    for d in range(N_DP):
        here = (block == ((d - group + N_DP) & 7)) & (inner < UNIT * count[d])
        target = jnp.where(here, UNIT * start[d] + inner, target)
    select = (target == lax.broadcasted_iota(jnp.int32, (192, 128), 1)).astype(F32).astype(BF16)
    moved = dot(select, home).astype(BF16).reshape(8, CAP, -1)
    for m, out in enumerate(outs):
        out[...] = moved[m]


def order_kernel(where_ref, *refs):
    group = 2 * where_ref[0] + where_ref[1]
    for m, ref in enumerate(refs[:-1]):
        refs[-1][(group - m + N_DP) & 7] = ref[...]


def body(tokens, tallies, membership, gain1, wqkv, sharp, wmerge, gain2, w1, w2):
    z, c, y, x = (lax.axis_index(name) for name in ("z", "c", "y", "x"))
    where = jnp.stack([z, c, y, x]).astype(jnp.int32)
    gain1 = gain1[None]
    gain2 = gain2[None]
    cy = ("c", "y")

    blocks = call(
        pick_kernel, [shape((32, 2048))] * 4, [SMEM, SMEM, VMEM], flops=10 * 10**9
    )(where, tallies, tokens)
    came = [blocks[0]] + [lax.ppermute(blocks[k], "y", ring(SIDE, k)) for k in (1, 2, 3)]
    w1_later, w2_later, _ = lax.optimization_barrier((w1, w2, blocks[1]))
    [mlp_slice] = call(
        slice_kernel,
        [shape((1024, 512))],
        [SMEM, ANY, ANY],
        [pltpu.SemaphoreType.DMA((5,))],
    )(where, w1_later, w2_later)
    near = lax.ppermute(mlp_slice, cy, twin_ring())
    column = jnp.concatenate(came, 0)
    arrived = [column] + [lax.ppermute(column, "x", ring(SIDE, m)) for m in (1, 2, 3)]
    near, _ = lax.optimization_barrier((near, column))
    near_all = lax.all_gather(near, DP, axis=0, tiled=False)
    [near_half] = call(half_kernel, [shape((512, 512))], [SMEM, VMEM])(where, near)
    far = lax.ppermute(near_half, cy, twin_ring())
    [packed] = call(
        pack_kernel,
        [shape((2064, 384))],
        [SMEM, ANY],
        [pltpu.SemaphoreType.DMA],
    )(sharp, lax.optimization_barrier((wqkv, column))[0])
    qkv_near = lax.ppermute(packed, cy, twin_ring())
    gain1, qkv_near, far = lax.optimization_barrier((gain1, qkv_near, far))
    normed, kept_rows = call(
        norm_kernel,
        [shape((512, 2048))] * 2,
        [ANY] * 4 + [VMEM],
        [pltpu.SemaphoreType.DMA((4,))],
        vmem=12,
        flops=25 * 10**9,
    )(*arrived, gain1)
    qkv_near2 = lax.ppermute(qkv_near, "c", ring(2, 1))
    [qkv_half] = call(far_kernel, [shape((1040, 384))], [SMEM, VMEM])(where, qkv_near)
    qkv_far = lax.ppermute(qkv_half, cy, twin_ring())

    [mine] = call(
        near_kernel,
        [shape((512, 256))],
        [SMEM] * 3 + [VMEM] + [ANY] * 2,
        [pltpu.VMEM((2064, 384), BF16)] * 2 + [pltpu.SemaphoreType.DMA((2,))],
        vmem=20,
        flops=2 * 10**9,
        moved=8 * 2**20,
    )(where, tallies, membership, normed, packed, qkv_near)
    qkv_far, mine = lax.optimization_barrier((qkv_far, mine))
    far, _ = lax.optimization_barrier((far, mine))
    far_all = lax.all_gather(far, DP, axis=0, tiled=False)
    qkv_far2 = lax.ppermute(qkv_far, "c", ring(2, 1))
    [mine_far] = call(
        far_attention_kernel,
        [shape((512, 256))],
        [SMEM] * 3 + [VMEM] + [ANY] * 3,
        [
            pltpu.VMEM((2064, 384), BF16),
            pltpu.VMEM((2, 1040, 384), BF16),
            pltpu.SemaphoreType.DMA((3,)),
        ],
        vmem=20,
        flops=2 * 10**9,
        moved=8 * 2**20,
    )(where, tallies, membership, normed, qkv_near2, qkv_far, qkv_far2)

    first = [mine] + [lax.ppermute(mine, "x", ring(SIDE, m)) for m in (1, 2, 3)]
    second = [mine_far] + [lax.ppermute(mine_far, "x", ring(SIDE, m)) for m in (1, 2, 3)]
    scratch = [pltpu.VMEM((1024, 2048), BF16), pltpu.VMEM((512, 1024), BF16)]
    [merged] = call(
        merge_first_kernel,
        [shape((512, 2048), F32)],
        [SMEM] + [VMEM] * 4 + [ANY] * 2,
        scratch + [pltpu.VMEM((512, 2048), BF16), pltpu.SemaphoreType.DMA((9,))],
        vmem=60,
        flops=2 * 10**9,
        moved=12 * 2**20,
    )(where, *first, kept_rows, wmerge)
    second[0], near_all = lax.optimization_barrier((second[0], near_all))
    fed, kept = call(
        merge_kernel,
        [shape((512, 2048)), shape((128, 2048), F32)],
        [SMEM] + [VMEM] * 5 + [ANY] * 2,
        scratch + [pltpu.VMEM((512, 2048), F32), pltpu.SemaphoreType.DMA((9,))],
        vmem=60,
        flops=25 * 10**9,
        moved=14 * 2**20,
    )(where, *second, gain2, merged, wmerge)

    [near_hidden] = call(
        near_mlp_kernel,
        [shape((512, 1536))],
        [VMEM] + [ANY] * 2,
        [pltpu.VMEM((3, 2048, 512), BF16), pltpu.SemaphoreType.DMA((3,))],
        vmem=60,
        flops=4 * 10**9,
        moved=10 * 2**20,
    )(fed, w1, near_all)
    [parts] = call(
        far_mlp_kernel,
        [shape((16, 32, 2048))],
        [SMEM, VMEM] + [ANY] * 5,
        [
            pltpu.VMEM((2048, 512), BF16),
            pltpu.VMEM((2048, 2048), BF16),
            pltpu.VMEM((512, 2048), BF16),
            pltpu.VMEM((128, 2048), F32),
            pltpu.SemaphoreType.DMA((6,)),
        ],
        vmem=60,
        flops=6 * 10**9,
        moved=14 * 2**20,
    )(where, fed, kept, near_hidden, w2, near_all, far_all)
    parts = lax.all_to_all(parts, ("y", "x"), 0, 0, tiled=True)
    leaving = call(leave_kernel, [shape((CAP, 2048))] * 8, [SMEM, SMEM, VMEM], vmem=14)(
        where, tallies, parts
    )
    got = [leaving[0]]
    got += [lax.ppermute(leaving[m], DP, ring(N_DP, m)) for m in range(1, N_DP)]
    [out] = call(order_kernel, [shape((N_DP, CAP, 2048))], [SMEM] + [VMEM] * 8)(where, *got)
    return out.reshape(N_DP * CAP, -1)


def solution(mesh):
    grid = Mesh(mesh.devices.reshape(4, 2, 4, 4), ("z", "c", "y", "x"))
    head = ("y", "x")
    in_specs = (
        P(DP + head, None),
        P(DP, None),
        P(DP, None),
        P(),
        P(None, head),
        P(head),
        P(),
        P(),
        P(None, head),
        P(head, None),
    )
    return jax.shard_map(
        body, mesh=grid, in_specs=in_specs, out_specs=P(DP + head, None), check_vma=False
    )
```

```python
import functools

import jax
import jax.numpy as jnp
from jax import lax
from jax.experimental import pallas as pl
from jax.experimental.pallas import tpu as pltpu
from jax.sharding import Mesh
from jax.sharding import PartitionSpec as P

HEAD_DIM = 128
UNIT = 8
N_DP = 8
SIDE = 4
CAP = 24
EPS = 1e-06
DP = ("z", "c")
BF16 = jnp.bfloat16
F32 = jnp.float32
VMEM = pl.BlockSpec(memory_space=pltpu.VMEM)
SMEM = pl.BlockSpec(memory_space=pltpu.SMEM)
ANY = pl.BlockSpec(memory_space=pl.ANY)


def ring(size, step):
    return [(i, (i + step) % size) for i in range(size)]


def twin_ring():
    down = [(y, (y - 1) % SIDE) for y in range(SIDE)]
    up = [(SIDE + y, SIDE + (y + 1) % SIDE) for y in range(SIDE)]
    return down + up


def dot(a, b):
    return jnp.dot(a, b, preferred_element_type=F32)


def shape(dims, dtype=BF16):
    return jax.ShapeDtypeStruct(dims, dtype)


def call(kernel, outs, ins, scratch=(), vmem=6, flops=0, moved=0):
    return pl.pallas_call(
        kernel,
        out_shape=outs,
        in_specs=ins,
        out_specs=[VMEM] * len(outs),
        scratch_shapes=list(scratch),
        compiler_params=pltpu.CompilerParams(vmem_limit_bytes=vmem * 2**20),
        cost_estimate=pl.CostEstimate(flops=flops, bytes_accessed=moved, transcendentals=0),
    )


def placement(count_ref, y):
    count = [count_ref[0, d] for d in range(N_DP)]
    offset, start, running = [], [], jnp.int32(0)
    for d in range(N_DP):
        offset.append(running)
        running = running + count[d]
        rank = jnp.int32(0)
        for e in range(N_DP):
            if e != d:
                ahead = count[e] >= count[d] if e < d else count[e] > count[d]
                rank = rank + ahead.astype(jnp.int32)
        place = jnp.where(rank < SIDE, 4 * rank, 4 * (7 - rank) + 4 - count[d])
        start.append((place - 4 * y + 16) & 15)
    return count, offset, start


def spread(unit, count, offset, values):
    out = jnp.zeros_like(unit)
    for d in range(N_DP):
        inside = (unit >= offset[d]) & (unit < offset[d] + count[d])
        out = out + jnp.where(inside, values[d], 0)
    return out


def pick_kernel(where_ref, count_ref, tokens_ref, *outs):
    count, offset, start = placement(count_ref, where_ref[2])
    row = lax.broadcasted_iota(jnp.int32, (1, 128), 1)
    unit = row >> 3
    place = unit + spread(unit, count, offset, [s - o for s, o in zip(start, offset)])
    target = place * UNIT + (row & 7)
    pick = (target == lax.broadcasted_iota(jnp.int32, (128, 128), 0)).astype(F32).astype(BF16)
    for n in range(4):
        cols = pl.ds(512 * n, 512)
        picked = dot(pick, tokens_ref[:, cols]).astype(BF16)
        for k in range(SIDE):
            outs[k][:, cols] = picked[32 * k : 32 * k + 32]


def slice_kernel(where_ref, w1_ref, w2_ref, out_ref, sem):
    z = where_ref[0]
    copies = [
        pltpu.make_async_copy(
            w1_ref.at[pl.ds(pl.multiple_of(z * 512, 512), 512)], out_ref.at[pl.ds(0, 512)], sem.at[0]
        )
    ]
    for q in range(4):
        copies.append(
            pltpu.make_async_copy(
                w2_ref.at[pl.ds(pl.multiple_of(z * 128, 128), 128), pl.ds(512 * q, 512)],
                out_ref.at[pl.ds(512 + 128 * q, 128)],
                sem.at[1 + q],
            )
        )
    for copy in copies:
        copy.start()
    for copy in copies:
        copy.wait()


def half_kernel(where_ref, got_ref, out_ref):
    c = where_ref[1]
    out_ref[:256] = got_ref[pl.ds(pl.multiple_of(c * 256, 256), 256)]
    for q in range(4):
        out_ref[256 + 64 * q : 320 + 64 * q] = got_ref[
            pl.ds(pl.multiple_of(512 + 128 * q + 64 * c, 64), 64)
        ]


def pack_kernel(sharp_ref, wqkv_ref, out_ref, sem):
    copy = pltpu.make_async_copy(wqkv_ref, out_ref.at[pl.ds(0, 2048)], sem)
    copy.start()
    value = jnp.full((16, 384), sharp_ref[0], F32)
    high = value.astype(BF16).astype(F32)
    mid = (value - high).astype(BF16).astype(F32)
    low = value - high - mid
    lane = lax.broadcasted_iota(jnp.int32, (16, 384), 1)
    terms = jnp.where(lane == 0, high, jnp.where(lane == 1, mid, jnp.where(lane == 2, low, 0.0)))
    out_ref[2048:] = terms.astype(BF16)
    copy.wait()


def far_kernel(where_ref, got_ref, out_ref):
    out_ref[:1024] = got_ref[pl.ds(pl.multiple_of(where_ref[1] * 1024, 1024), 1024)]
    out_ref[1024:] = got_ref[2048:]


def unit_norm(values):
    mean_square = jnp.mean(values * values, axis=-1, keepdims=True)
    return (values * lax.rsqrt(mean_square + EPS) * HEAD_DIM ** (-0.5)).astype(BF16)


def key_of_place(count_ref, member_ref, y):
    count, offset, start = placement(count_ref, y)
    row = (lax.broadcasted_iota(jnp.int32, (1, 512), 1) >> 3) & 3
    col = (lax.broadcasted_iota(jnp.int32, (512, 1), 0) >> 3) & 3
    key_row = jnp.zeros((1, 512), jnp.int32)
    key_col = jnp.zeros((512, 1), jnp.int32)
    for p in range(4):
        key = jnp.int32(0)
        for d in range(N_DP):
            inside = (start[d] <= p) & (p < start[d] + count[d])
            member = member_ref[0, jnp.where(inside, offset[d] + p - start[d], 0)]
            key = key + jnp.where(inside, d * 4 + member, 0)
        key_row = key_row + jnp.where(row == p, key, 0)
        key_col = key_col + jnp.where(col == p, key, 0)
    return key_col == key_row


def attend(raw, scale_row, allowed):
    q = unit_norm(raw[:, :128])
    k = unit_norm(raw[:, 128:256])
    v = raw[:, 256:].astype(BF16)
    score = lax.dot_general(q, k, (((1,), (1,)), ((), ())), preferred_element_type=F32)
    scale = jnp.sum(scale_row.astype(F32), axis=-1, keepdims=True)
    score = jnp.where(allowed, score * scale, -1e30)
    weights = jnp.exp(score - jnp.max(score, axis=-1, keepdims=True))
    p = (weights * (1.0 / jnp.sum(weights, axis=-1, keepdims=True))).astype(BF16)
    return dot(p, v).astype(BF16)


def norm_kernel(a0, a1, a2, a3, gain_ref, out_ref, kept_ref, sem):
    copies = [
        pltpu.make_async_copy(ref, kept_ref.at[pl.ds(128 * j, 128)], sem.at[j])
        for j, ref in enumerate((a0, a1, a2, a3))
    ]
    for copy in copies:
        copy.start()
    for j, copy in enumerate(copies):
        rows = slice(128 * j, 128 * j + 128)
        copy.wait()
        values = kept_ref[rows].astype(F32)
        mean_square = jnp.mean(values * values, axis=-1, keepdims=True)
        out_ref[rows] = (values * lax.rsqrt(mean_square + EPS) * gain_ref[...]).astype(BF16)


def near_kernel(where_ref, count_ref, member_ref, xn, wq0, wq1, out_ref, w0, w1, sem):
    copies = [
        pltpu.make_async_copy(src, dst, sem.at[i])
        for i, (src, dst) in enumerate(((wq0, w0), (wq1, w1)))
    ]
    for copy in copies:
        copy.start()
    allowed = key_of_place(count_ref, member_ref, where_ref[2])
    for k, w in enumerate((w0, w1)):
        copies[k].wait()
        raw = dot(xn[...], w[:2048])
        out_ref[:, 128 * k : 128 * k + 128] = attend(raw, w[2048:2049], allowed)


def far_attention_kernel(where_ref, count_ref, member_ref, xn, wq2, wqa, wqb, out_ref, w2, w3, sem):
    c = where_ref[1]
    copies = [
        pltpu.make_async_copy(wq2, w2, sem.at[0]),
        pltpu.make_async_copy(wqa, w3.at[c], sem.at[1]),
        pltpu.make_async_copy(wqb, w3.at[1 - c], sem.at[2]),
    ]
    for copy in copies:
        copy.start()
    allowed = key_of_place(count_ref, member_ref, where_ref[2])
    copies[0].wait()
    out_ref[:, :128] = attend(dot(xn[...], w2[:2048]), w2[2048:2049], allowed)
    copies[1].wait()
    copies[2].wait()
    raw = dot(xn[:, :1024], w3[0, :1024]) + dot(xn[:, 1024:], w3[1, :1024])
    out_ref[:, 128:] = attend(raw, w3[0, 1024:1025], allowed)


def merge_part(where_ref, refs, wm_ref, wm, heads, sem):
    c, y, x = where_ref[1], where_ref[2], where_ref[3]
    step = 1 - 2 * c
    source = [y, (y + step + 4) & 3]
    copies = []
    for m in range(SIDE):
        for k in range(2):
            head = source[k] * SIDE + ((x - m + 4) & 3)
            copies.append(
                pltpu.make_async_copy(
                    wm_ref.at[pl.ds(pl.multiple_of(head * HEAD_DIM, HEAD_DIM), HEAD_DIM)],
                    wm.at[pl.ds(256 * m + HEAD_DIM * k, HEAD_DIM)],
                    sem.at[2 * m + k],
                )
            )
    for copy in copies:
        copy.start()
    for m, ref in enumerate(refs):
        for j in range(SIDE):
            theirs = 128 * ((j - m) % SIDE)
            heads[128 * j : 128 * j + 128, 256 * m : 256 * m + 256] = ref[theirs : theirs + 128]
    for copy in copies:
        copy.wait()


def merge_first_kernel(where_ref, o0, o1, o2, o3, rows_ref, wm_ref, out_ref, wm, heads, rows, sem):
    carried = pltpu.make_async_copy(rows_ref, rows, sem.at[8])
    carried.start()
    merge_part(where_ref, (o0, o1, o2, o3), wm_ref, wm, heads, sem)
    carried.wait()
    for n in range(4):
        cols = slice(512 * n, 512 * n + 512)
        out_ref[:, cols] = dot(heads[...], wm[:, cols]) + rows[:, cols].astype(F32)


def merge_kernel(
    where_ref, f0, f1, f2, f3, gain_ref, part_ref, wm_ref, w1_ref, all_ref,
    fed_ref, kept_ref, out_ref, wm, heads, total, w1, sem,
):
    c, y, x = where_ref[1], where_ref[2], where_ref[3]
    step = 1 - 2 * c
    source = [(y - step + 4) & 3, (y + 2) & 3]
    merges = []
    for n in range(4):
        cols = pl.ds(512 * n, 512)
        group = [pltpu.make_async_copy(part_ref.at[:, cols], total.at[:, cols], sem.at[n])]
        for m in range(SIDE):
            for k in range(2):
                head = source[k] * SIDE + ((x - m + 4) & 3)
                rows = pl.ds(pl.multiple_of(head * HEAD_DIM, HEAD_DIM), HEAD_DIM)
                here = pl.ds(256 * m + HEAD_DIM * k, HEAD_DIM)
                group.append(
                    pltpu.make_async_copy(wm_ref.at[rows, cols], wm.at[here, cols], sem.at[n])
                )
        merges.append(group)
    ups = [[pltpu.make_async_copy(w1_ref, w1.at[0], sem.at[4])]]
    for half in range(2):
        ups.append(
            [
                pltpu.make_async_copy(
                    all_ref.at[2 * z + half, pl.ds(0, 512)],
                    w1.at[1 + half, pl.ds(512 * z, 512)],
                    sem.at[5 + half],
                )
                for z in range(4)
            ]
        )
    for group in merges + ups:
        for copy in group:
            copy.start()
    for m, ref in enumerate((f0, f1, f2, f3)):
        for j in range(SIDE):
            theirs = 128 * ((j - m) % SIDE)
            heads[128 * j : 128 * j + 128, 256 * m : 256 * m + 256] = ref[theirs : theirs + 128]
    squares = jnp.zeros((512, 1), F32)
    for n in range(4):
        cols = slice(512 * n, 512 * n + 512)
        for copy in merges[n]:
            copy.wait()
        part = dot(heads[...], wm[:, cols]) + total[:, cols]
        squares = squares + jnp.sum(part * part, axis=-1, keepdims=True)
        total[:, cols] = part
    scale = lax.rsqrt(squares * (1.0 / 2048) + EPS)
    for n in range(4):
        cols = slice(512 * n, 512 * n + 512)
        fed_ref[:, cols] = (total[:, cols] * scale * gain_ref[:, cols]).astype(BF16)
    kept_ref[...] = total[:128]
    for i in range(3):
        for copy in ups[i]:
            copy.wait()
        out_ref[:, 512 * i : 512 * i + 512] = jax.nn.gelu(
            dot(fed_ref[...], w1[i]), approximate=True
        ).astype(BF16)


def far_mlp_kernel(
    where_ref, fed_ref, kept_ref, hidden_ref, w2_ref, near_ref, far_ref, out_ref,
    w1, w2, hidden, kept, sem,
):
    ups, downs = [], []
    for z in range(4):
        for c in range(2):
            block = far_ref.at[2 * z + c]
            ups.append(
                pltpu.make_async_copy(
                    block.at[pl.ds(0, 256)], w1.at[pl.ds(512 * z + 256 * c, 256)], sem.at[0]
                )
            )
    carried = [
        pltpu.make_async_copy(hidden_ref, hidden.at[:, pl.ds(0, 1536)], sem.at[1]),
        pltpu.make_async_copy(kept_ref, kept, sem.at[1]),
    ]
    for n in range(4):
        cols = pl.ds(512 * n, 512)
        down = [pltpu.make_async_copy(w2_ref.at[:, cols], w2.at[pl.ds(0, 512), cols], sem.at[2 + n])]
        for c in range(2):
            for z in range(4):
                down.append(
                    pltpu.make_async_copy(
                        near_ref.at[2 * z + c, pl.ds(512 + 128 * n, 128)],
                        w2.at[pl.ds(512 * (1 + c) + 128 * z, 128), cols],
                        sem.at[2 + n],
                    )
                )
                down.append(
                    pltpu.make_async_copy(
                        far_ref.at[2 * z + c, pl.ds(256 + 64 * n, 64)],
                        w2.at[pl.ds(1536 + 128 * z + 64 * c, 64), cols],
                        sem.at[2 + n],
                    )
                )
        downs.append(down)
    for copies in [ups, carried, *downs]:
        for copy in copies:
            copy.start()
    for copy in ups:
        copy.wait()
    hidden[:, 1536:] = jax.nn.gelu(dot(fed_ref[...], w1[...]), approximate=True).astype(BF16)
    for copy in carried:
        copy.wait()
    for n in range(4):
        cols = slice(512 * n, 512 * n + 512)
        for copy in downs[n]:
            copy.wait()
        part = dot(hidden[...], w2[:, cols])
        for j in range(SIDE):
            for k in range(SIDE):
                rows = slice(128 * j + 32 * k, 128 * j + 32 * k + 32)
                home = ((where_ref[2] - k + 4) & 3) * SIDE + ((where_ref[3] - j + 4) & 3)
                block = part[rows]
                if j == 0:
                    block = block + kept[rows, cols]
                out_ref[home, :, cols] = block.astype(BF16)


def leave_kernel(where_ref, count_ref, parts_ref, *outs):
    group = 2 * where_ref[0] + where_ref[1]
    count, _, start = placement(count_ref, 0)
    slot = lax.broadcasted_iota(jnp.int32, (192, 1), 0)
    block = slot // CAP
    inner = slot - block * CAP
    rows = []
    for y in range(SIDE):
        total = parts_ref[4 * y].astype(F32)
        for x in range(1, SIDE):
            total = total + parts_ref[4 * y + x].astype(F32)
        rows.append(total.astype(BF16))
    home = jnp.concatenate(rows, 0)
    target = jnp.full((192, 1), -1, jnp.int32)
    for d in range(N_DP):
        here = (block == ((d - group + N_DP) & 7)) & (inner < UNIT * count[d])
        target = jnp.where(here, UNIT * start[d] + inner, target)
    select = (target == lax.broadcasted_iota(jnp.int32, (192, 128), 1)).astype(F32).astype(BF16)
    moved = dot(select, home).astype(BF16).reshape(8, CAP, -1)
    for m, out in enumerate(outs):
        out[...] = moved[m]


def order_kernel(where_ref, *refs):
    group = 2 * where_ref[0] + where_ref[1]
    for m, ref in enumerate(refs[:-1]):
        refs[-1][(group - m + N_DP) & 7] = ref[...]


def body(tokens, tallies, membership, gain1, wqkv, sharp, wmerge, gain2, w1, w2):
    z, c, y, x = (lax.axis_index(name) for name in ("z", "c", "y", "x"))
    where = jnp.stack([z, c, y, x]).astype(jnp.int32)
    gain1 = gain1[None]
    gain2 = gain2[None]
    cy = ("c", "y")

    blocks = call(
        pick_kernel, [shape((32, 2048))] * 4, [SMEM, SMEM, VMEM], flops=10 * 10**9
    )(where, tallies, tokens)
    came = [blocks[0]] + [lax.ppermute(blocks[k], "y", ring(SIDE, k)) for k in (1, 2, 3)]
    w1_later, w2_later, _ = lax.optimization_barrier((w1, w2, blocks[1]))
    [mlp_slice] = call(
        slice_kernel,
        [shape((1024, 512))],
        [SMEM, ANY, ANY],
        [pltpu.SemaphoreType.DMA((5,))],
    )(where, w1_later, w2_later)
    near = lax.ppermute(mlp_slice, cy, twin_ring())
    column = jnp.concatenate(came, 0)
    arrived = [column] + [lax.ppermute(column, "x", ring(SIDE, m)) for m in (1, 2, 3)]
    near, _ = lax.optimization_barrier((near, column))
    near_all = lax.all_gather(near, DP, axis=0, tiled=False)
    [near_half] = call(half_kernel, [shape((512, 512))], [SMEM, VMEM])(where, near)
    far = lax.ppermute(near_half, cy, twin_ring())
    [packed] = call(
        pack_kernel,
        [shape((2064, 384))],
        [SMEM, ANY],
        [pltpu.SemaphoreType.DMA],
    )(sharp, lax.optimization_barrier((wqkv, column))[0])
    qkv_near = lax.ppermute(packed, cy, twin_ring())
    gain1, qkv_near, far = lax.optimization_barrier((gain1, qkv_near, far))
    normed, kept_rows = call(
        norm_kernel,
        [shape((512, 2048))] * 2,
        [ANY] * 4 + [VMEM],
        [pltpu.SemaphoreType.DMA((4,))],
        vmem=12,
        flops=25 * 10**9,
    )(*arrived, gain1)
    qkv_near2 = lax.ppermute(qkv_near, "c", ring(2, 1))
    [qkv_half] = call(far_kernel, [shape((1040, 384))], [SMEM, VMEM])(where, qkv_near)
    qkv_far = lax.ppermute(qkv_half, cy, twin_ring())

    [mine] = call(
        near_kernel,
        [shape((512, 256))],
        [SMEM] * 3 + [VMEM] + [ANY] * 2,
        [pltpu.VMEM((2064, 384), BF16)] * 2 + [pltpu.SemaphoreType.DMA((2,))],
        vmem=20,
        flops=2 * 10**9,
        moved=8 * 2**20,
    )(where, tallies, membership, normed, packed, qkv_near)
    qkv_far, mine = lax.optimization_barrier((qkv_far, mine))
    far, _ = lax.optimization_barrier((far, mine))
    far_all = lax.all_gather(far, DP, axis=0, tiled=False)
    qkv_far2 = lax.ppermute(qkv_far, "c", ring(2, 1))
    [mine_far] = call(
        far_attention_kernel,
        [shape((512, 256))],
        [SMEM] * 3 + [VMEM] + [ANY] * 3,
        [
            pltpu.VMEM((2064, 384), BF16),
            pltpu.VMEM((2, 1040, 384), BF16),
            pltpu.SemaphoreType.DMA((3,)),
        ],
        vmem=20,
        flops=2 * 10**9,
        moved=8 * 2**20,
    )(where, tallies, membership, normed, qkv_near2, qkv_far, qkv_far2)

    first = [mine] + [lax.ppermute(mine, "x", ring(SIDE, m)) for m in (1, 2, 3)]
    second = [mine_far] + [lax.ppermute(mine_far, "x", ring(SIDE, m)) for m in (1, 2, 3)]
    scratch = [pltpu.VMEM((1024, 2048), BF16), pltpu.VMEM((512, 1024), BF16)]
    [merged] = call(
        merge_first_kernel,
        [shape((512, 2048), F32)],
        [SMEM] + [VMEM] * 4 + [ANY] * 2,
        scratch + [pltpu.VMEM((512, 2048), BF16), pltpu.SemaphoreType.DMA((9,))],
        vmem=60,
        flops=2 * 10**9,
        moved=12 * 2**20,
    )(where, *first, kept_rows, wmerge)
    second[0], near_all = lax.optimization_barrier((second[0], near_all))
    fed, kept, near_hidden = call(
        merge_kernel,
        [shape((512, 2048)), shape((128, 2048), F32), shape((512, 1536))],
        [SMEM] + [VMEM] * 5 + [ANY] * 4,
        scratch
        + [
            pltpu.VMEM((512, 2048), F32),
            pltpu.VMEM((3, 2048, 512), BF16),
            pltpu.SemaphoreType.DMA((7,)),
        ],
        vmem=60,
        flops=25 * 10**9,
        moved=24 * 2**20,
    )(where, *second, gain2, merged, wmerge, w1, near_all)

    [parts] = call(
        far_mlp_kernel,
        [shape((16, 32, 2048))],
        [SMEM, VMEM] + [ANY] * 5,
        [
            pltpu.VMEM((2048, 512), BF16),
            pltpu.VMEM((2048, 2048), BF16),
            pltpu.VMEM((512, 2048), BF16),
            pltpu.VMEM((128, 2048), F32),
            pltpu.SemaphoreType.DMA((6,)),
        ],
        vmem=60,
        flops=6 * 10**9,
        moved=14 * 2**20,
    )(where, fed, kept, near_hidden, w2, near_all, far_all)
    parts = lax.all_to_all(parts, ("y", "x"), 0, 0, tiled=True)
    leaving = call(leave_kernel, [shape((CAP, 2048))] * 8, [SMEM, SMEM, VMEM], vmem=14)(
        where, tallies, parts
    )
    got = [leaving[0]]
    got += [lax.ppermute(leaving[m], DP, ring(N_DP, m)) for m in range(1, N_DP)]
    [out] = call(order_kernel, [shape((N_DP, CAP, 2048))], [SMEM] + [VMEM] * 8)(where, *got)
    return out.reshape(N_DP * CAP, -1)


def solution(mesh):
    grid = Mesh(mesh.devices.reshape(4, 2, 4, 4), ("z", "c", "y", "x"))
    head = ("y", "x")
    in_specs = (
        P(DP + head, None),
        P(DP, None),
        P(DP, None),
        P(),
        P(None, head),
        P(head),
        P(),
        P(),
        P(None, head),
        P(head, None),
    )
    return jax.shard_map(
        body, mesh=grid, in_specs=in_specs, out_specs=P(DP + head, None), check_vma=False
    )
```

```python
import functools

import jax
import jax.numpy as jnp
from jax import lax
from jax.experimental import pallas as pl
from jax.experimental.pallas import tpu as pltpu
from jax.sharding import Mesh
from jax.sharding import PartitionSpec as P

HEAD_DIM = 128
UNIT = 8
N_DP = 8
SIDE = 4
CAP = 24
EPS = 1e-06
DP = ("z", "c")
BF16 = jnp.bfloat16
F32 = jnp.float32
VMEM = pl.BlockSpec(memory_space=pltpu.VMEM)
SMEM = pl.BlockSpec(memory_space=pltpu.SMEM)
ANY = pl.BlockSpec(memory_space=pl.ANY)


def ring(size, step):
    return [(i, (i + step) % size) for i in range(size)]


def twin_ring():
    down = [(y, (y - 1) % SIDE) for y in range(SIDE)]
    up = [(SIDE + y, SIDE + (y + 1) % SIDE) for y in range(SIDE)]
    return down + up


def dot(a, b):
    return jnp.dot(a, b, preferred_element_type=F32)


def shape(dims, dtype=BF16):
    return jax.ShapeDtypeStruct(dims, dtype)


def call(kernel, outs, ins, scratch=(), vmem=6, flops=0, moved=0):
    return pl.pallas_call(
        kernel,
        out_shape=outs,
        in_specs=ins,
        out_specs=[VMEM] * len(outs),
        scratch_shapes=list(scratch),
        compiler_params=pltpu.CompilerParams(vmem_limit_bytes=vmem * 2**20),
        cost_estimate=pl.CostEstimate(flops=flops, bytes_accessed=moved, transcendentals=0),
    )


def placement(count_ref, y):
    count = [count_ref[0, d] for d in range(N_DP)]
    offset, start, running = [], [], jnp.int32(0)
    for d in range(N_DP):
        offset.append(running)
        running = running + count[d]
        rank = jnp.int32(0)
        for e in range(N_DP):
            if e != d:
                ahead = count[e] >= count[d] if e < d else count[e] > count[d]
                rank = rank + ahead.astype(jnp.int32)
        place = jnp.where(rank < SIDE, 4 * rank, 4 * (7 - rank) + 4 - count[d])
        start.append((place - 4 * y + 16) & 15)
    return count, offset, start


def spread(unit, count, offset, values):
    out = jnp.zeros_like(unit)
    for d in range(N_DP):
        inside = (unit >= offset[d]) & (unit < offset[d] + count[d])
        out = out + jnp.where(inside, values[d], 0)
    return out


def pick_kernel(where_ref, count_ref, tokens_ref, *outs):
    count, offset, start = placement(count_ref, where_ref[2])
    row = lax.broadcasted_iota(jnp.int32, (1, 128), 1)
    unit = row >> 3
    place = unit + spread(unit, count, offset, [s - o for s, o in zip(start, offset)])
    target = place * UNIT + (row & 7)
    pick = (target == lax.broadcasted_iota(jnp.int32, (128, 128), 0)).astype(F32).astype(BF16)
    for n in range(4):
        cols = pl.ds(512 * n, 512)
        picked = dot(pick, tokens_ref[:, cols]).astype(BF16)
        for k in range(SIDE):
            outs[k][:, cols] = picked[32 * k : 32 * k + 32]


def slice_kernel(where_ref, w1_ref, w2_ref, out_ref, sem):
    z = where_ref[0]
    copies = [
        pltpu.make_async_copy(
            w1_ref.at[pl.ds(pl.multiple_of(z * 512, 512), 512)], out_ref.at[pl.ds(0, 512)], sem.at[0]
        )
    ]
    for q in range(4):
        copies.append(
            pltpu.make_async_copy(
                w2_ref.at[pl.ds(pl.multiple_of(z * 128, 128), 128), pl.ds(512 * q, 512)],
                out_ref.at[pl.ds(512 + 128 * q, 128)],
                sem.at[1 + q],
            )
        )
    for copy in copies:
        copy.start()
    for copy in copies:
        copy.wait()


def half_kernel(where_ref, got_ref, out_ref):
    c = where_ref[1]
    out_ref[:256] = got_ref[pl.ds(pl.multiple_of(c * 256, 256), 256)]
    for q in range(4):
        out_ref[256 + 64 * q : 320 + 64 * q] = got_ref[
            pl.ds(pl.multiple_of(512 + 128 * q + 64 * c, 64), 64)
        ]


def pack_kernel(sharp_ref, wqkv_ref, out_ref, sem):
    copy = pltpu.make_async_copy(wqkv_ref, out_ref.at[pl.ds(0, 2048)], sem)
    copy.start()
    value = jnp.full((16, 384), sharp_ref[0], F32)
    high = value.astype(BF16).astype(F32)
    mid = (value - high).astype(BF16).astype(F32)
    low = value - high - mid
    lane = lax.broadcasted_iota(jnp.int32, (16, 384), 1)
    terms = jnp.where(lane == 0, high, jnp.where(lane == 1, mid, jnp.where(lane == 2, low, 0.0)))
    out_ref[2048:] = terms.astype(BF16)
    copy.wait()


def far_kernel(where_ref, got_ref, out_ref):
    out_ref[:1024] = got_ref[pl.ds(pl.multiple_of(where_ref[1] * 1024, 1024), 1024)]
    out_ref[1024:] = got_ref[2048:]


def unit_norm(values):
    mean_square = jnp.mean(values * values, axis=-1, keepdims=True)
    return (values * lax.rsqrt(mean_square + EPS) * HEAD_DIM ** (-0.5)).astype(BF16)


def key_of_place(count_ref, member_ref, y):
    count, offset, start = placement(count_ref, y)
    row = (lax.broadcasted_iota(jnp.int32, (1, 512), 1) >> 3) & 3
    col = (lax.broadcasted_iota(jnp.int32, (512, 1), 0) >> 3) & 3
    key_row = jnp.zeros((1, 512), jnp.int32)
    key_col = jnp.zeros((512, 1), jnp.int32)
    for p in range(4):
        key = jnp.int32(0)
        for d in range(N_DP):
            inside = (start[d] <= p) & (p < start[d] + count[d])
            member = member_ref[0, jnp.where(inside, offset[d] + p - start[d], 0)]
            key = key + jnp.where(inside, d * 4 + member, 0)
        key_row = key_row + jnp.where(row == p, key, 0)
        key_col = key_col + jnp.where(col == p, key, 0)
    return key_col == key_row


def attend(raw, scale_row, allowed):
    q = unit_norm(raw[:, :128])
    k = unit_norm(raw[:, 128:256])
    v = raw[:, 256:].astype(BF16)
    score = lax.dot_general(q, k, (((1,), (1,)), ((), ())), preferred_element_type=F32)
    scale = jnp.sum(scale_row.astype(F32), axis=-1, keepdims=True)
    score = jnp.where(allowed, score * scale, -1e30)
    weights = jnp.exp(score - jnp.max(score, axis=-1, keepdims=True))
    p = (weights * (1.0 / jnp.sum(weights, axis=-1, keepdims=True))).astype(BF16)
    return dot(p, v).astype(BF16)


def norm_kernel(a0, a1, a2, a3, gain_ref, out_ref, kept_ref, sem):
    copies = [
        pltpu.make_async_copy(ref, kept_ref.at[pl.ds(128 * j, 128)], sem.at[j])
        for j, ref in enumerate((a0, a1, a2, a3))
    ]
    for copy in copies:
        copy.start()
    for j, copy in enumerate(copies):
        rows = slice(128 * j, 128 * j + 128)
        copy.wait()
        values = kept_ref[rows].astype(F32)
        mean_square = jnp.mean(values * values, axis=-1, keepdims=True)
        out_ref[rows] = (values * lax.rsqrt(mean_square + EPS) * gain_ref[...]).astype(BF16)


def near_kernel(where_ref, count_ref, member_ref, xn, wq0, wq1, out_ref, w0, w1, sem):
    copies = [
        pltpu.make_async_copy(src, dst, sem.at[i])
        for i, (src, dst) in enumerate(((wq0, w0), (wq1, w1)))
    ]
    for copy in copies:
        copy.start()
    allowed = key_of_place(count_ref, member_ref, where_ref[2])
    for k, w in enumerate((w0, w1)):
        copies[k].wait()
        raw = dot(xn[...], w[:2048])
        out_ref[:, 128 * k : 128 * k + 128] = attend(raw, w[2048:2049], allowed)


def far_attention_kernel(where_ref, count_ref, member_ref, xn, wq2, wqa, wqb, out_ref, w2, w3, sem):
    c = where_ref[1]
    copies = [
        pltpu.make_async_copy(wq2, w2, sem.at[0]),
        pltpu.make_async_copy(wqa, w3.at[c], sem.at[1]),
        pltpu.make_async_copy(wqb, w3.at[1 - c], sem.at[2]),
    ]
    for copy in copies:
        copy.start()
    allowed = key_of_place(count_ref, member_ref, where_ref[2])
    copies[0].wait()
    out_ref[:, :128] = attend(dot(xn[...], w2[:2048]), w2[2048:2049], allowed)
    copies[1].wait()
    copies[2].wait()
    raw = dot(xn[:, :1024], w3[0, :1024]) + dot(xn[:, 1024:], w3[1, :1024])
    out_ref[:, 128:] = attend(raw, w3[0, 1024:1025], allowed)


def merge_part(where_ref, refs, wm_ref, wm, heads, sem):
    c, y, x = where_ref[1], where_ref[2], where_ref[3]
    step = 1 - 2 * c
    source = [y, (y + step + 4) & 3]
    copies = []
    for m in range(SIDE):
        for k in range(2):
            head = source[k] * SIDE + ((x - m + 4) & 3)
            copies.append(
                pltpu.make_async_copy(
                    wm_ref.at[pl.ds(pl.multiple_of(head * HEAD_DIM, HEAD_DIM), HEAD_DIM)],
                    wm.at[pl.ds(256 * m + HEAD_DIM * k, HEAD_DIM)],
                    sem.at[2 * m + k],
                )
            )
    for copy in copies:
        copy.start()
    for m, ref in enumerate(refs):
        for j in range(SIDE):
            theirs = 128 * ((j - m) % SIDE)
            heads[128 * j : 128 * j + 128, 256 * m : 256 * m + 256] = ref[theirs : theirs + 128]
    for copy in copies:
        copy.wait()


def merge_first_kernel(where_ref, o0, o1, o2, o3, rows_ref, wm_ref, out_ref, wm, heads, rows, sem):
    carried = pltpu.make_async_copy(rows_ref, rows, sem.at[8])
    carried.start()
    merge_part(where_ref, (o0, o1, o2, o3), wm_ref, wm, heads, sem)
    carried.wait()
    for n in range(4):
        cols = slice(512 * n, 512 * n + 512)
        out_ref[:, cols] = dot(heads[...], wm[:, cols]) + rows[:, cols].astype(F32)


def merge_kernel(
    where_ref, f0, f1, f2, f3, gain_ref, part_ref, wm_ref, w1_ref, w2_ref, all_ref,
    fed_ref, sums_ref, wm, heads, total, w1, w2, hidden, sem,
):
    c, y, x = where_ref[1], where_ref[2], where_ref[3]
    step = 1 - 2 * c
    source = [(y - step + 4) & 3, (y + 2) & 3]
    merges = []
    for n in range(4):
        cols = pl.ds(512 * n, 512)
        group = [pltpu.make_async_copy(part_ref.at[:, cols], total.at[:, cols], sem.at[n])]
        for m in range(SIDE):
            for k in range(2):
                head = source[k] * SIDE + ((x - m + 4) & 3)
                rows = pl.ds(pl.multiple_of(head * HEAD_DIM, HEAD_DIM), HEAD_DIM)
                here = pl.ds(256 * m + HEAD_DIM * k, HEAD_DIM)
                group.append(
                    pltpu.make_async_copy(wm_ref.at[rows, cols], wm.at[here, cols], sem.at[n])
                )
        merges.append(group)
    ups = [[pltpu.make_async_copy(w1_ref, w1.at[0], sem.at[4])]]
    for half in range(2):
        ups.append(
            [
                pltpu.make_async_copy(
                    all_ref.at[2 * z + half, pl.ds(0, 512)],
                    w1.at[1 + half, pl.ds(512 * z, 512)],
                    sem.at[5 + half],
                )
                for z in range(4)
            ]
        )
    downs = []
    for n in range(4):
        cols = pl.ds(512 * n, 512)
        down = [pltpu.make_async_copy(w2_ref.at[:, cols], w2.at[pl.ds(0, 512), cols], sem.at[7 + n])]
        for half in range(2):
            for z in range(4):
                down.append(
                    pltpu.make_async_copy(
                        all_ref.at[2 * z + half, pl.ds(512 + 128 * n, 128)],
                        w2.at[pl.ds(512 * (1 + half) + 128 * z, 128), cols],
                        sem.at[7 + n],
                    )
                )
        downs.append(down)
    for group in merges + ups + downs:
        for copy in group:
            copy.start()
    for m, ref in enumerate((f0, f1, f2, f3)):
        for j in range(SIDE):
            theirs = 128 * ((j - m) % SIDE)
            heads[128 * j : 128 * j + 128, 256 * m : 256 * m + 256] = ref[theirs : theirs + 128]
    squares = jnp.zeros((512, 1), F32)
    for n in range(4):
        cols = slice(512 * n, 512 * n + 512)
        for copy in merges[n]:
            copy.wait()
        part = dot(heads[...], wm[:, cols]) + total[:, cols]
        squares = squares + jnp.sum(part * part, axis=-1, keepdims=True)
        total[:, cols] = part
    scale = lax.rsqrt(squares * (1.0 / 2048) + EPS)
    for n in range(4):
        cols = slice(512 * n, 512 * n + 512)
        fed_ref[:, cols] = (total[:, cols] * scale * gain_ref[:, cols]).astype(BF16)
    for i in range(3):
        for copy in ups[i]:
            copy.wait()
        hidden[:, 512 * i : 512 * i + 512] = jax.nn.gelu(
            dot(fed_ref[...], w1[i]), approximate=True
        ).astype(BF16)
    for n in range(4):
        cols = slice(512 * n, 512 * n + 512)
        for copy in downs[n]:
            copy.wait()
        part = dot(hidden[...], w2[:, cols])
        sums_ref[:128, cols] = total[:128, cols] + part[:128]
        sums_ref[128:, cols] = part[128:]


def far_mlp_kernel(where_ref, fed_ref, part_ref, all_ref, out_ref, w1, w2, sums, sem):
    ups, downs = [], []
    for z in range(4):
        for c in range(2):
            block = all_ref.at[2 * z + c]
            ups.append(
                pltpu.make_async_copy(
                    block.at[pl.ds(0, 256)], w1.at[pl.ds(512 * z + 256 * c, 256)], sem.at[0]
                )
            )
            for n in range(4):
                downs.append(
                    pltpu.make_async_copy(
                        block.at[pl.ds(256 + 64 * n, 64)],
                        w2.at[pl.ds(128 * z + 64 * c, 64), pl.ds(512 * n, 512)],
                        sem.at[1],
                    )
                )
    carried = pltpu.make_async_copy(part_ref, sums, sem.at[2])
    for copy in [*ups, *downs, carried]:
        copy.start()
    for copy in ups:
        copy.wait()
    hidden = jax.nn.gelu(dot(fed_ref[...], w1[...]), approximate=True).astype(BF16)
    for copy in [*downs, carried]:
        copy.wait()
    for n in range(4):
        cols = slice(512 * n, 512 * n + 512)
        part = sums[:, cols] + dot(hidden, w2[:, cols])
        for j in range(SIDE):
            for k in range(SIDE):
                rows = slice(128 * j + 32 * k, 128 * j + 32 * k + 32)
                home = ((where_ref[2] - k + 4) & 3) * SIDE + ((where_ref[3] - j + 4) & 3)
                out_ref[home, :, cols] = part[rows].astype(BF16)


def leave_kernel(where_ref, count_ref, parts_ref, *outs):
    group = 2 * where_ref[0] + where_ref[1]
    count, _, start = placement(count_ref, 0)
    slot = lax.broadcasted_iota(jnp.int32, (192, 1), 0)
    block = slot // CAP
    inner = slot - block * CAP
    rows = []
    for y in range(SIDE):
        total = parts_ref[4 * y].astype(F32)
        for x in range(1, SIDE):
            total = total + parts_ref[4 * y + x].astype(F32)
        rows.append(total.astype(BF16))
    home = jnp.concatenate(rows, 0)
    target = jnp.full((192, 1), -1, jnp.int32)
    for d in range(N_DP):
        here = (block == ((d - group + N_DP) & 7)) & (inner < UNIT * count[d])
        target = jnp.where(here, UNIT * start[d] + inner, target)
    select = (target == lax.broadcasted_iota(jnp.int32, (192, 128), 1)).astype(F32).astype(BF16)
    moved = dot(select, home).astype(BF16).reshape(8, CAP, -1)
    for m, out in enumerate(outs):
        out[...] = moved[m]


def order_kernel(where_ref, *refs):
    group = 2 * where_ref[0] + where_ref[1]
    for m, ref in enumerate(refs[:-1]):
        refs[-1][(group - m + N_DP) & 7] = ref[...]


def body(tokens, tallies, membership, gain1, wqkv, sharp, wmerge, gain2, w1, w2):
    z, c, y, x = (lax.axis_index(name) for name in ("z", "c", "y", "x"))
    where = jnp.stack([z, c, y, x]).astype(jnp.int32)
    gain1 = gain1[None]
    gain2 = gain2[None]
    cy = ("c", "y")

    blocks = call(
        pick_kernel, [shape((32, 2048))] * 4, [SMEM, SMEM, VMEM], flops=10 * 10**9
    )(where, tallies, tokens)
    came = [blocks[0]] + [lax.ppermute(blocks[k], "y", ring(SIDE, k)) for k in (1, 2, 3)]
    w1_later, w2_later, _ = lax.optimization_barrier((w1, w2, blocks[1]))
    [mlp_slice] = call(
        slice_kernel,
        [shape((1024, 512))],
        [SMEM, ANY, ANY],
        [pltpu.SemaphoreType.DMA((5,))],
    )(where, w1_later, w2_later)
    near = lax.ppermute(mlp_slice, cy, twin_ring())
    column = jnp.concatenate(came, 0)
    arrived = [column] + [lax.ppermute(column, "x", ring(SIDE, m)) for m in (1, 2, 3)]
    near, _ = lax.optimization_barrier((near, column))
    near_all = lax.all_gather(near, DP, axis=0, tiled=False)
    [near_half] = call(half_kernel, [shape((512, 512))], [SMEM, VMEM])(where, near)
    far = lax.ppermute(near_half, cy, twin_ring())
    [packed] = call(
        pack_kernel,
        [shape((2064, 384))],
        [SMEM, ANY],
        [pltpu.SemaphoreType.DMA],
    )(sharp, lax.optimization_barrier((wqkv, column))[0])
    qkv_near = lax.ppermute(packed, cy, twin_ring())
    gain1, qkv_near, far = lax.optimization_barrier((gain1, qkv_near, far))
    normed, kept_rows = call(
        norm_kernel,
        [shape((512, 2048))] * 2,
        [ANY] * 4 + [VMEM],
        [pltpu.SemaphoreType.DMA((4,))],
        vmem=12,
        flops=25 * 10**9,
    )(*arrived, gain1)
    qkv_near2 = lax.ppermute(qkv_near, "c", ring(2, 1))
    [qkv_half] = call(far_kernel, [shape((1040, 384))], [SMEM, VMEM])(where, qkv_near)
    qkv_far = lax.ppermute(qkv_half, cy, twin_ring())

    [mine] = call(
        near_kernel,
        [shape((512, 256))],
        [SMEM] * 3 + [VMEM] + [ANY] * 2,
        [pltpu.VMEM((2064, 384), BF16)] * 2 + [pltpu.SemaphoreType.DMA((2,))],
        vmem=20,
        flops=2 * 10**9,
        moved=8 * 2**20,
    )(where, tallies, membership, normed, packed, qkv_near)
    qkv_far, mine = lax.optimization_barrier((qkv_far, mine))
    far, _ = lax.optimization_barrier((far, mine))
    far_all = lax.all_gather(far, DP, axis=0, tiled=False)
    qkv_far2 = lax.ppermute(qkv_far, "c", ring(2, 1))
    [mine_far] = call(
        far_attention_kernel,
        [shape((512, 256))],
        [SMEM] * 3 + [VMEM] + [ANY] * 3,
        [
            pltpu.VMEM((2064, 384), BF16),
            pltpu.VMEM((2, 1040, 384), BF16),
            pltpu.SemaphoreType.DMA((3,)),
        ],
        vmem=20,
        flops=2 * 10**9,
        moved=8 * 2**20,
    )(where, tallies, membership, normed, qkv_near2, qkv_far, qkv_far2)

    first = [mine] + [lax.ppermute(mine, "x", ring(SIDE, m)) for m in (1, 2, 3)]
    second = [mine_far] + [lax.ppermute(mine_far, "x", ring(SIDE, m)) for m in (1, 2, 3)]
    scratch = [pltpu.VMEM((1024, 2048), BF16), pltpu.VMEM((512, 1024), BF16)]
    [merged] = call(
        merge_first_kernel,
        [shape((512, 2048), F32)],
        [SMEM] + [VMEM] * 4 + [ANY] * 2,
        scratch + [pltpu.VMEM((512, 2048), BF16), pltpu.SemaphoreType.DMA((9,))],
        vmem=60,
        flops=2 * 10**9,
        moved=12 * 2**20,
    )(where, *first, kept_rows, wmerge)
    second[0], near_all = lax.optimization_barrier((second[0], near_all))
    fed, near_part = call(
        merge_kernel,
        [shape((512, 2048)), shape((512, 2048), F32)],
        [SMEM] + [VMEM] * 5 + [ANY] * 5,
        scratch
        + [
            pltpu.VMEM((512, 2048), F32),
            pltpu.VMEM((3, 2048, 512), BF16),
            pltpu.VMEM((1536, 2048), BF16),
            pltpu.VMEM((512, 1536), BF16),
            pltpu.SemaphoreType.DMA((11,)),
        ],
        vmem=60,
        flops=25 * 10**9,
        moved=34 * 2**20,
    )(where, *second, gain2, merged, wmerge, w1, w2, near_all)

    [parts] = call(
        far_mlp_kernel,
        [shape((16, 32, 2048))],
        [SMEM, VMEM] + [ANY] * 2,
        [
            pltpu.VMEM((2048, 512), BF16),
            pltpu.VMEM((512, 2048), BF16),
            pltpu.VMEM((512, 2048), F32),
            pltpu.SemaphoreType.DMA((3,)),
        ],
        vmem=60,
        flops=2 * 10**9,
        moved=10 * 2**20,
    )(where, fed, near_part, far_all)
    parts = lax.all_to_all(parts, ("y", "x"), 0, 0, tiled=True)
    leaving = call(leave_kernel, [shape((CAP, 2048))] * 8, [SMEM, SMEM, VMEM], vmem=14)(
        where, tallies, parts
    )
    got = [leaving[0]]
    got += [lax.ppermute(leaving[m], DP, ring(N_DP, m)) for m in range(1, N_DP)]
    [out] = call(order_kernel, [shape((N_DP, CAP, 2048))], [SMEM] + [VMEM] * 8)(where, *got)
    return out.reshape(N_DP * CAP, -1)


def solution(mesh):
    grid = Mesh(mesh.devices.reshape(4, 2, 4, 4), ("z", "c", "y", "x"))
    head = ("y", "x")
    in_specs = (
        P(DP + head, None),
        P(DP, None),
        P(DP, None),
        P(),
        P(None, head),
        P(head),
        P(),
        P(),
        P(None, head),
        P(head, None),
    )
    return jax.shard_map(
        body, mesh=grid, in_specs=in_specs, out_specs=P(DP + head, None), check_vma=False
    )
```
